32 devices in a mesh: groups: 1, expert: 8 (over z, y), fsdp: 2 (over x), dp: 2 (over core).
Axes of the slice: x: 2, y: 2, z: 4, core: 2. Of those that a mesh axis runs over, the one named last changes fastest.
Arguments:
- moe_input: bfloat16 [4096, 1024], P(('groups', 'expert', 'fsdp', 'dp')), may hold values from -6 to 6
- moe_gain: float32 [1024], replicated, may hold values from 0.2 to 2
- routes: int32 [4096, 10], P(('groups', 'expert', 'fsdp', 'dp')), may hold values from 0 to 31, all different within a row; in each aligned block of 128 rows (0 to 127, 128 to 255, ...) at most 50 rows name the same one
- route_gates: float32 [4096, 10], P(('groups', 'expert', 'fsdp', 'dp')), may hold values from 0.05 to 0.2
- expert_gate: bfloat16 [32, 1024, 512], P(('expert', 'dp'), None, 'fsdp'), may hold values from -0.1875 to 0.1875
- expert_up: bfloat16 [32, 1024, 512], P(('expert', 'dp'), None, 'fsdp'), may hold values from -0.1875 to 0.1875
- expert_down: bfloat16 [32, 512, 1024], P(('expert', 'dp'), 'fsdp'), may hold values from -0.25 to 0.25
- shared_gate: bfloat16 [1024, 512], P(None, 'fsdp'), may hold values from -0.1875 to 0.1875
- shared_up: bfloat16 [1024, 512], P(None, 'fsdp'), may hold values from -0.1875 to 0.1875
- shared_down: bfloat16 [512, 1024], P('fsdp'), may hold values from -0.25 to 0.25
- shared_switch: float32 [1024], replicated, may hold values from -0.5 to 0.5
- mixed_qkv: bfloat16 [32, 128, 4096], P(('groups', 'expert', 'fsdp', 'dp')), may hold values from -6 to 6
- out_gate: bfloat16 [32, 128, 2048], P(('groups', 'expert', 'fsdp', 'dp')), may hold values from -6 to 6
- beta_logit: float32 [32, 128, 16], P(('groups', 'expert', 'fsdp', 'dp')), may hold values from -6 to 6
- step_logit: float32 [32, 128, 16], P(('groups', 'expert', 'fsdp', 'dp')), may hold values from -6 to 6
- conv_weight: float32 [4, 4096], replicated, may hold values from -3 to 3
- decay_log: float32 [16], replicated, may hold values from -3 to 1.5
- decay_bias: float32 [16], replicated, may hold values from -2 to 2
- head_gain: float32 [128], replicated, may hold values from 0.2 to 2
- lengths: int32 [32], P(('groups', 'expert', 'fsdp', 'dp')), may hold values from 32 to 128, as said below
Outputs:
- moe_output: bfloat16 [4096, 1024], P(('groups', 'expert', 'fsdp', 'dp'))
- core_output: bfloat16 [32, 128, 2048], P(('groups', 'expert', 'fsdp', 'dp'))
The draws below stay inside these ranges and needn't reach their ends.
Inputs may be any that keep to these rules, and one draw needn't show every extreme that they name: `routes`: the rows of one device name each expert at most 50 times, a bound that some block reaches. `lengths`: some request is live at all 128 positions.
All inputs are finite; a program needn't handle non-finite values.
Results may differ from the reference program's by a relative error of at most 0.0069.
Values may be sent and summed in bfloat16 or wider, within the bound.
A program may use at most 128 MiB of HBM per device.

```python
import math
import jax
import jax.numpy as jnp
import numpy as np
from jax import lax

D = 1024
H = 512
FS = 512
TOPK = 10
TOK_DEV = 128
SEQ = 128
VHEADS = 16
HEAD = 128
CONV = 4
EXPERTS = 32
CAP = 50
TOKENS = 4096
NREQ = 32
QKV = 4096
N_EXPERT = 8
N_FSDP = 2
N_DP = 2


def draw_lengths(key, part):
    key = jax.random.fold_in(key, 7)
    key_lengths, key_full = jax.random.split(key)
    drawn_lengths = jax.random.randint(key_lengths, (NREQ,), SEQ // 4, SEQ + 1, dtype=jnp.int32)
    where_full = jax.random.randint(key_full, (), 0, NREQ, dtype=jnp.int32)
    return drawn_lengths.at[where_full].set(SEQ)


def level_of(rng, dims, cuts, smallest, top_value):
    level = 1.0
    for axis_at, blocks in cuts:
        heights = jax.random.uniform(jax.random.fold_in(jax.random.fold_in(rng, 6), axis_at), (blocks,), jnp.float32, smallest / len(cuts), top_value / len(cuts))
        level = level * jnp.repeat(jnp.exp(heights), dims[axis_at] // blocks).reshape((-1,) + (1,) * (len(dims) - 1 - axis_at))
    return level


def routed_block(rng, own, number, rows, amount, top, reach, lean):
    ranking = jax.random.permutation(rng, amount)
    packed, usual = shares(amount, rows * top, reach, lean, True), shares(amount, rows * top, reach, lean, False)
    places = jnp.arange(amount)

    def named(sizes, turn):
        used = int((sizes > 0).sum())
        fixed = max(1, used // 4)
        passed = fixed + (places - fixed + turn * (used - fixed)) % max(1, amount - fixed)
        return jnp.zeros((amount,), jnp.int32).at[ranking[jnp.where(places < fixed, places, passed)]].set(jnp.asarray(sizes, jnp.int32))

    sizes = jnp.where(number % 4 == 0, named(packed, number // 4), named(usual, number - number // 4 - 1))
    mixed = jax.random.permutation(jax.random.fold_in(own, 3), amount)
    donor, taker = mixed[0:amount // 2 * 2:2], mixed[1:amount // 2 * 2:2]
    margin = jnp.minimum(sizes[donor] - 1, reach - sizes[taker]) // 2
    margin = jnp.where((donor == ranking[0]) | (taker == ranking[0]) | (sizes[taker] == 0), 0, jnp.maximum(margin, 0))
    passed = jax.random.randint(jax.random.fold_in(own, 4), (amount // 2,), 0, 1 << 20) % (margin + 1)
    sizes = sizes.at[donor].add(-passed).at[taker].add(passed)
    members = jnp.searchsorted(jnp.cumsum(sizes), jnp.arange(rows * top), side="right").astype(jnp.int32)
    table = members.reshape(top, rows).T
    table = table[jax.random.permutation(jax.random.fold_in(own, 1), rows)]
    turn = jax.random.randint(jax.random.fold_in(own, 2), (rows, 1), 0, top)
    return jnp.take_along_axis(table, (jnp.arange(top)[None, :] + turn) % top, axis=1)


def shares(count, total, reach, slope, full):
    portions = [(1 << 20) // math.isqrt(grade ** slope) + 1 for grade in range(1, count + 1)]
    largest = reach if full else min(reach, max(-(-total // count), total * portions[0] // sum(portions)))
    least = 1 if total - largest >= count - 1 else 0
    given, rest = [largest] + [least] * (count - 1), total - largest - least * (count - 1)
    while rest > 0:
        free = [i for i in range(1, count) if given[i] < largest] or [i for i in range(1, count) if given[i] < reach]
        mass, left = sum([portions[i] for i in free]), rest
        for i in free:
            addition = min(reach - given[i], max(1, left * portions[i] // mass), rest)
            given[i] = given[i] + addition
            rest = rest - addition
    return np.array(given)


def normal_values(rng, extent, deviation, most, shards=(), kind=jnp.bfloat16):
    array = jax.random.normal(rng, extent, jnp.float32) * deviation
    if len(shards) > 0:
        array = level_of(rng, extent, shards, -0.22, 0.18) * array
    return jnp.clip(array, min=-most, max=most).astype(kind)


def setup_inputs(seed: int = 0, part: int = 0) -> dict:
    splits = jax.random.split(jax.random.key(seed), 21)
    part_splits = jax.random.split(jax.random.fold_in(splits[20], part), 21)
    moe_input = normal_values(part_splits[0], (TOKENS, D), 1.0, 6.0, ((0, 32),))
    moe_gain = jnp.clip(jax.random.uniform(splits[1], (D,), jnp.float32, 0.2, 2.0), 0.2, 2.0)
    routes_keys = jax.random.split(jax.random.fold_in(part_splits[2], 1), TOKENS // TOK_DEV)
    routes_turns = jax.random.permutation(jax.random.fold_in(part_splits[2], 3), TOKENS // TOK_DEV)
    routes = jax.vmap(lambda own, number: routed_block(jax.random.fold_in(part_splits[2], 2), own, number, TOK_DEV, EXPERTS, TOPK, CAP, 1))(routes_keys, routes_turns).reshape((TOKENS, TOPK))
    route_gates = jnp.clip(0.05 + 0.15 * jax.random.uniform(part_splits[3], (TOKENS, TOPK), jnp.float32) ** level_of(part_splits[3], (TOKENS, TOPK), ((0, 32),), -0.2, 0.2), 0.05, 0.2)
    expert_gate = normal_values(splits[4], (EXPERTS, D, H), D ** -0.5, 0.1875, ((0, 16), (2, 2)))
    expert_up = normal_values(splits[5], (EXPERTS, D, H), D ** -0.5, 0.1875, ((0, 16), (2, 2)))
    expert_down = normal_values(splits[6], (EXPERTS, H, D), H ** -0.5, 0.25, ((0, 16), (1, 2)))
    shared_gate = normal_values(splits[7], (D, FS), D ** -0.5, 0.1875, ((1, 2),))
    shared_up = normal_values(splits[8], (D, FS), D ** -0.5, 0.1875, ((1, 2),))
    shared_down = normal_values(splits[9], (FS, D), FS ** -0.5, 0.25, ((0, 2),))
    shared_switch = normal_values(splits[10], (D,), (D // 9) ** -0.5, 0.5, (), jnp.float32)
    mixed_qkv = normal_values(part_splits[11], (NREQ, SEQ, QKV), 1.0, 6.0, ((0, 32),))
    out_gate = normal_values(part_splits[12], (NREQ, SEQ, VHEADS * HEAD), 1.0, 6.0, ((0, 32),))
    beta_logit = normal_values(part_splits[13], (NREQ, SEQ, VHEADS), 1.5, 6.0, ((0, 32),), jnp.float32)
    step_logit = normal_values(part_splits[14], (NREQ, SEQ, VHEADS), 1.0, 6.0, ((0, 32),), jnp.float32)
    conv_weight = normal_values(splits[15], (CONV, QKV), CONV ** -0.5, 3.0, (), jnp.float32)
    decay_log = jnp.clip(jax.random.uniform(splits[16], (VHEADS,), jnp.float32, -3.0, 1.5), -3.0, 1.5)
    decay_bias = jnp.clip(jax.random.uniform(splits[17], (VHEADS,), jnp.float32, -2.0, 2.0), -2.0, 2.0)
    head_gain = jnp.clip(jax.random.uniform(splits[18], (HEAD,), jnp.float32, 0.2, 2.0), 0.2, 2.0)
    lengths = draw_lengths(jax.random.fold_in(jax.random.fold_in(splits[20], part), 71), part)
    return {"moe_input": moe_input, "moe_gain": moe_gain, "routes": routes, "route_gates": route_gates, "expert_gate": expert_gate, "expert_up": expert_up, "expert_down": expert_down, "shared_gate": shared_gate, "shared_up": shared_up, "shared_down": shared_down, "shared_switch": shared_switch, "mixed_qkv": mixed_qkv, "out_gate": out_gate, "beta_logit": beta_logit, "step_logit": step_logit, "conv_weight": conv_weight, "decay_log": decay_log, "decay_bias": decay_bias, "head_gain": head_gain, "lengths": lengths}


EPS = 1e-06
HIGHEST = lax.Precision.HIGHEST

def normalize_rows(rows, gain):
    widened = rows.astype(jnp.float32)
    factor = lax.rsqrt(lax.optimization_barrier(jnp.mean(widened * widened, axis=-1, keepdims=True)) + EPS)
    return widened * factor * gain

def expert_rows(rows, w_gate, w_up, w_down):
    gate_part = jnp.dot(rows, w_gate, preferred_element_type=jnp.float32)
    up_part = jnp.dot(rows, w_up, preferred_element_type=jnp.float32)
    hidden = (jax.nn.silu(gate_part) * up_part).astype(jnp.bfloat16)
    return jnp.dot(hidden, w_down, preferred_element_type=jnp.float32)

def conv_silu(streams, conv_weight):
    widened = streams.astype(jnp.float32)
    kernel_size = conv_weight.shape[0]
    length = widened.shape[1]
    padded = jnp.pad(widened, ((0, 0), (kernel_size - 1, 0), (0, 0)))
    summed = jnp.zeros_like(widened)
    for offset in range(kernel_size):
        summed = summed + conv_weight[offset] * padded[:, offset:offset + length]
    return jax.nn.silu(summed)

def unit_vectors(vectors):
    return vectors * lax.rsqrt(lax.optimization_barrier(jnp.sum(vectors * vectors, axis=-1, keepdims=True)) + EPS)

def prepare_heads(mixed_qkv, beta_logit, step_logit, conv_weight, decay_log, decay_bias, head_gain):
    streams = conv_silu(mixed_qkv, conv_weight)
    batch_count, length, channels = streams.shape
    head_size = head_gain.shape[0]
    value_heads = decay_log.shape[0]
    key_heads = (channels - value_heads * head_size) // (2 * head_size)
    key_span = key_heads * head_size
    queries = unit_vectors(streams[:, :, :key_span].reshape(batch_count, length, key_heads, head_size))
    queries = queries * (1.0 / math.sqrt(head_size))
    keys_all = unit_vectors(streams[:, :, key_span:2 * key_span].reshape(batch_count, length, key_heads, head_size))
    values = streams[:, :, 2 * key_span:].reshape(batch_count, length, value_heads, head_size)
    repeat = value_heads // key_heads
    queries = jnp.repeat(queries, repeat, axis=2)
    keys_all = jnp.repeat(keys_all, repeat, axis=2)
    beta_gate = jax.nn.sigmoid(beta_logit)
    decays = -jnp.exp(decay_log) * jax.nn.softplus(step_logit + decay_bias)
    return (queries, keys_all, values, beta_gate, decays)

def gated_output(attended, out_gate, head_gain, lengths):
    batch_count, length, heads_count, head_size = attended.shape
    normed = normalize_rows(attended, head_gain)
    gate_now = out_gate.astype(jnp.float32).reshape(batch_count, length, heads_count, head_size)
    gated_rows = (normed * jax.nn.silu(gate_now)).reshape(batch_count, length, heads_count * head_size)
    positions = jnp.arange(length, dtype=jnp.int32)
    live_mask = positions[None, :] < lengths[:, None]
    return jnp.where(live_mask[:, :, None], gated_rows, 0.0).astype(jnp.bfloat16)

def recurrence(queries, keys_all, values, beta_gate, decays):
    batch_count, length, heads_count, head_size = queries.shape

    def advance(memory, inputs):
        query_now, key_now, value_now, beta_now, decay_now = inputs
        memory = memory * jnp.exp(decay_now)[..., None, None]
        recalled = jnp.einsum('nhd,nhde->nhe', key_now, memory, precision=HIGHEST)
        correction = (value_now - recalled) * beta_now[..., None]
        memory = memory + key_now[..., :, None] * correction[..., None, :]
        return (memory, jnp.einsum('nhd,nhde->nhe', query_now, memory, precision=HIGHEST))
    zero_state = jnp.zeros((batch_count, heads_count, head_size, head_size), jnp.float32)
    time_major = tuple((jnp.swapaxes(tensor_in, 0, 1) for tensor_in in (queries, keys_all, values, beta_gate, decays)))
    final_memory, attended = lax.scan(advance, zero_state, time_major)
    return jnp.swapaxes(attended, 0, 1)

def reference(moe_input, moe_gain, routes, route_gates, expert_gate, expert_up, expert_down, shared_gate, shared_up, shared_down, shared_switch, mixed_qkv, out_gate, beta_logit, step_logit, conv_weight, decay_log, decay_bias, head_gain, lengths):
    normed = normalize_rows(moe_input, moe_gain).astype(jnp.bfloat16)
    token_count, features = normed.shape
    flat_routes = routes.reshape(-1).astype(jnp.int32)
    route_count = flat_routes.shape[0]
    order = jnp.argsort(flat_routes, stable=True).astype(jnp.int32)
    ordered = flat_routes[order]
    starts = jnp.searchsorted(ordered, jnp.arange(EXPERTS, dtype=jnp.int32)).astype(jnp.int32)
    rank_in = jnp.arange(route_count, dtype=jnp.int32) - starts[ordered]
    most_rows = N_EXPERT * N_FSDP * N_DP * CAP
    table = jnp.full((EXPERTS, most_rows), route_count, jnp.int32).at[ordered, rank_in].set(order)
    padded_rows = jnp.concatenate([normed, jnp.zeros((1, features), jnp.bfloat16)], axis=0)
    weights = jnp.concatenate([route_gates.reshape(-1), jnp.zeros((1,), jnp.float32)], axis=0)

    def one_expert(running, index):
        picks = table[index]
        token_ids = jnp.where(picks < route_count, picks // TOPK, token_count).astype(jnp.int32)
        produced = expert_rows(padded_rows[token_ids], expert_gate[index], expert_up[index], expert_down[index]).astype(jnp.bfloat16)
        term = weights[picks][:, None] * produced.astype(jnp.float32)
        return (running.at[token_ids].add(term), None)
    running, unused = lax.scan(one_expert, jnp.zeros((token_count + 1, features), jnp.float32), jnp.arange(EXPERTS, dtype=jnp.int32))
    shared_result = expert_rows(normed, shared_gate, shared_up, shared_down)
    switch = jax.nn.sigmoid(jnp.dot(normed.astype(jnp.float32), shared_switch, precision=HIGHEST))
    moe_output = (running[:token_count] + switch[:, None] * shared_result).astype(jnp.bfloat16)
    queries, keys_all, values, beta_gate, decays = prepare_heads(mixed_qkv, beta_logit, step_logit, conv_weight, decay_log, decay_bias, head_gain)
    attended = recurrence(queries, keys_all, values, beta_gate, decays)
    core_output = gated_output(attended, out_gate, head_gain, lengths)
    return (moe_output, core_output)
```

```python
import functools
import math

import jax
import jax.numpy as jnp
from jax import lax
from jax.experimental import pallas as pl
from jax.experimental.pallas import tpu as pltpu
from jax.sharding import PartitionSpec as P

EPS = 1e-06
HIGHEST = lax.Precision.HIGHEST


def normalize_rows(rows, gain):
    widened = rows.astype(jnp.float32)
    factor = lax.rsqrt(jnp.mean(widened * widened, axis=-1, keepdims=True) + EPS)
    return widened * factor * gain


def expert_rows(rows, w_gate, w_up, w_down):
    gate_part = jnp.dot(rows, w_gate, preferred_element_type=jnp.float32)
    up_part = jnp.dot(rows, w_up, preferred_element_type=jnp.float32)
    hidden = (jax.nn.silu(gate_part) * up_part).astype(jnp.bfloat16)
    return jnp.dot(hidden, w_down, preferred_element_type=jnp.float32)


def split_bf16(value):
    high = value.astype(jnp.bfloat16)
    low = (value - high.astype(jnp.float32)).astype(jnp.bfloat16)
    return high, low


def product(left, right):
    width = right.shape[1]
    lefts = jnp.concatenate(split_bf16(left), axis=1)
    rights = jnp.concatenate(split_bf16(right), axis=1)
    rights = jnp.concatenate([rights, rights], axis=0)
    both = jnp.dot(lefts, rights, preferred_element_type=jnp.float32)
    return both[:, :width] + both[:, width:]


def product_nt(left, right):
    width = right.shape[0]
    lefts = jnp.concatenate(split_bf16(left), axis=1)
    rights = jnp.concatenate(split_bf16(right), axis=0)
    rights = jnp.concatenate([rights, rights], axis=1)
    both = lax.dot_general(
        lefts, rights, (((1,), (1,)), ((), ())), preferred_element_type=jnp.float32
    )
    return both[:, :width] + both[:, width:]


def sigmoid(value):
    return 1.0 / (1.0 + jnp.exp(-value))


def conv_rows(rows, taps):
    widened = rows.astype(jnp.float32)
    count = taps.shape[0]
    position = lax.broadcasted_iota(jnp.int32, widened.shape, 0)
    total = taps[count - 1 : count, :] * widened
    for back in range(1, count):
        moved = jnp.where(position >= back, pltpu.roll(widened, back, 0), 0.0)
        total = total + taps[count - 1 - back : count - back, :] * moved
    return total * sigmoid(total)


def unit_rows(rows):
    return rows * lax.rsqrt(jnp.sum(rows * rows, axis=-1, keepdims=True) + EPS)


def mixer_prepare(beta_ref, step_ref, log_ref, bias_ref, run_t_ref, run_ref, gate_ref):
    length, heads = step_ref.shape
    row = lax.broadcasted_iota(jnp.int32, (length, length), 0)
    col = lax.broadcasted_iota(jnp.int32, (length, length), 1)
    step = step_ref[...] + bias_ref[...]
    softplus = jnp.maximum(step, 0.0) + jnp.log1p(jnp.exp(-jnp.abs(step)))
    decay = -jnp.exp(log_ref[...]) * softplus
    lower = jnp.where(row >= col, 1.0, 0.0).astype(jnp.bfloat16)
    high, low = split_bf16(decay)
    rest = (decay - high.astype(jnp.float32) - low.astype(jnp.float32)).astype(jnp.bfloat16)
    running = jnp.zeros((length, heads), jnp.float32)
    for piece in (rest, low, high):
        running = running + jnp.dot(lower, piece, preferred_element_type=jnp.float32)
    padded = jnp.concatenate(
        [running, jnp.zeros((length, length - heads), jnp.float32)], axis=1
    )
    run_ref[...] = padded
    run_t_ref[...] = jnp.transpose(padded)
    gate_ref[...] = jnp.concatenate(
        [sigmoid(beta_ref[...]), jnp.zeros((length, length - heads), jnp.float32)], axis=1
    )


def mixer_group(
    group, key_heads, total_heads, repeat, size,
    qkv_ref, gate_in_ref, taps_ref, gain_ref, live, run_t_ref, run_ref, gate_ref, out_ref,
):
    length = qkv_ref.shape[0]
    span = key_heads * size
    wide = span * repeat

    def columns(base, width):
        return pl.ds(pl.multiple_of(base + group * width, size), width)

    row = lax.broadcasted_iota(jnp.int32, (length, length), 0)
    col = lax.broadcasted_iota(jnp.int32, (length, length), 1)
    q_cols = columns(0, span)
    k_cols = columns(total_heads * size, span)
    v_cols = columns(2 * total_heads * size, wide)
    queries = conv_rows(qkv_ref[:, q_cols], taps_ref[:, q_cols])
    keys = conv_rows(qkv_ref[:, k_cols], taps_ref[:, k_cols])
    values = conv_rows(qkv_ref[:, v_cols], taps_ref[:, v_cols])
    running_all, gates_all = run_ref[...], gate_ref[...]
    systems, scores, targets = [], [], []
    for key_head in range(key_heads):
        here = slice(key_head * size, (key_head + 1) * size)
        query = unit_rows(queries[:, here]) * (1.0 / math.sqrt(size))
        key = unit_rows(keys[:, here])
        both = product_nt(jnp.concatenate([query, key], axis=0), key)
        for part in range(repeat):
            local_head = key_head * repeat + part
            head = group * (key_heads * repeat) + local_head
            run_col = jnp.sum(jnp.where(col == head, running_all, 0.0), axis=1, keepdims=True)
            beta = jnp.sum(jnp.where(col == head, gates_all, 0.0), axis=1, keepdims=True)
            run_row = run_t_ref[pl.ds(head, 1), :]
            spread = jnp.where(row >= col, run_col - run_row, 0.0)
            factors = jnp.where(row >= col, jnp.exp(spread), 0.0)
            scores.append(both[:length] * factors)
            systems.append(jnp.where(row > col, beta * both[length:] * factors, 0.0))
            targets.append(beta * values[:, local_head * size : (local_head + 1) * size])
    eye = jnp.where(row == col, 1.0, 0.0)
    block = 8
    near = (row // block) == (col // block)
    firsts = [jnp.where(near, system, 0.0) for system in systems]
    seconds = [product(first, first) for first in firsts]
    fourths = [product(second, second) for second in seconds]
    inverses = [
        eye - first + second - product(first, second) for first, second in zip(firsts, seconds)
    ]
    inverses = [
        inverse + product(inverse, fourth) for inverse, fourth in zip(inverses, fourths)
    ]
    while block < length:
        joined = ((row // (2 * block)) == (col // (2 * block))) & ((row // block) != (col // block))
        links = [jnp.where(joined, system, 0.0) for system in systems]
        halves = [product(link, inverse) for link, inverse in zip(links, inverses)]
        inverses = [
            inverse - product(inverse, half) for inverse, half in zip(inverses, halves)
        ]
        block = 2 * block
    updates = [product(inverse, target) for inverse, target in zip(inverses, targets)]
    results = [product(score, update) for score, update in zip(scores, updates)]
    position = lax.broadcasted_iota(jnp.int32, (length, size), 0)
    for local_head, attended in enumerate(results):
        head = group * (key_heads * repeat) + local_head
        head_cols = pl.ds(pl.multiple_of(head * size, size), size)
        factor = lax.rsqrt(jnp.mean(attended * attended, axis=-1, keepdims=True) + EPS)
        gate = gate_in_ref[:, head_cols].astype(jnp.float32)
        gated = attended * factor * gain_ref[...] * (gate * sigmoid(gate))
        out_ref[:, head_cols] = jnp.where(position < live, gated, 0.0).astype(jnp.bfloat16)


def mixer_kernel(
    key_heads, total_heads, repeat, size,
    live_ref, qkv_ref, gate_in_ref, beta_ref, step_ref, taps_ref, log_ref, bias_ref, gain_ref,
    out_ref, run_t_ref, run_ref, gate_ref,
):
    request = pl.program_id(0)
    mixer_prepare(beta_ref, step_ref, log_ref, bias_ref, run_t_ref, run_ref, gate_ref)

    @pl.loop(0, total_heads // key_heads)
    def _(group):
        mixer_group(
            group, key_heads, total_heads, repeat, size,
            qkv_ref, gate_in_ref, taps_ref, gain_ref, live_ref[request],
            run_t_ref, run_ref, gate_ref, out_ref,
        )


def mixer(
    mixed_qkv, out_gate, beta_logit, step_logit, conv_weight, decay_log, decay_bias, head_gain, lengths
):
    requests, length, channels = mixed_qkv.shape
    heads = decay_log.shape[0]
    size = head_gain.shape[0]
    total_heads = (channels - heads * size) // (2 * size)
    repeat = heads // total_heads

    def whole(array):
        return pl.BlockSpec(array.shape, lambda r: (0,) * array.ndim)

    def one(array):
        return pl.BlockSpec((None,) + array.shape[1:], lambda r: (r, 0, 0))

    small = [conv_weight, decay_log[None, :], decay_bias[None, :], head_gain[None, :]]
    return pl.pallas_call(
        functools.partial(mixer_kernel, 2, total_heads, repeat, size),
        grid=(requests,),
        out_shape=jax.ShapeDtypeStruct(out_gate.shape, jnp.bfloat16),
        in_specs=[pl.BlockSpec(memory_space=pltpu.SMEM)]
        + [one(array) for array in (mixed_qkv, out_gate, beta_logit, step_logit)]
        + [whole(array) for array in small],
        out_specs=one(out_gate),
        scratch_shapes=[pltpu.VMEM((length, length), jnp.float32)] * 3,
        compiler_params=pltpu.CompilerParams(vmem_limit_bytes=32 * 1024 * 1024),
        cost_estimate=pl.CostEstimate(
            flops=20_000_000_000, bytes_accessed=4_000_000, transcendentals=0
        ),
    )(lengths, mixed_qkv, out_gate, beta_logit, step_logit, *small)


def dense_experts(
    normed, routes, route_gates, expert_gate, expert_up, expert_down,
    shared_gate, shared_up, shared_down, shared_switch,
):
    tokens, features = normed.shape
    ways = ("expert", "fsdp")
    experts = lax.axis_size("expert") * lax.axis_size("dp") * expert_gate.shape[0]
    names = jnp.arange(experts, dtype=jnp.int32)
    share = jnp.sum(
        jnp.where(routes[:, :, None] == names, route_gates[:, :, None], 0.0), axis=1
    )
    high, low = split_bf16(share)
    pad = jnp.zeros((tokens, 128 - 2 * experts), jnp.bfloat16)
    rows = jnp.concatenate([normed, high, low, pad], axis=1)
    rows = lax.all_gather(rows, ways, axis=0, tiled=True)
    gate = lax.all_gather(expert_gate, "dp", axis=0, tiled=True)
    up = lax.all_gather(expert_up, "dp", axis=0, tiled=True)
    down = lax.all_gather(expert_down, "dp", axis=0, tiled=True)
    held = gate.shape[0]
    first = lax.axis_index("expert") * held
    shares = lax.dynamic_slice_in_dim(rows, features + first, held, 1).astype(
        jnp.float32
    ) + lax.dynamic_slice_in_dim(rows, features + experts + first, held, 1).astype(jnp.float32)
    every = rows[:, :features]
    gates = jnp.einsum("td,edh->teh", every, gate, preferred_element_type=jnp.float32)
    ups = jnp.einsum("td,edh->teh", every, up, preferred_element_type=jnp.float32)
    hidden = (jax.nn.silu(gates) * ups * shares[:, :, None]).astype(jnp.bfloat16)
    partial = jnp.einsum("teh,ehd->td", hidden, down, preferred_element_type=jnp.float32)
    near = lax.axis_size("fsdp") * tokens
    start = lax.axis_index("expert") * near
    mine = lax.dynamic_slice_in_dim(every, start, near, 0)
    switch = jax.nn.sigmoid(jnp.dot(mine.astype(jnp.float32), shared_switch, precision=HIGHEST))
    shared = switch[:, None] * expert_rows(mine, shared_gate, shared_up, shared_down)
    partial = lax.dynamic_update_slice_in_dim(
        partial, lax.dynamic_slice_in_dim(partial, start, near, 0) + shared, start, 0
    ).astype(jnp.bfloat16)
    return lax.psum_scatter(partial, ways, scatter_dimension=0, tiled=True)


def local(
    moe_input,
    moe_gain,
    routes,
    route_gates,
    expert_gate,
    expert_up,
    expert_down,
    shared_gate,
    shared_up,
    shared_down,
    shared_switch,
    mixed_qkv,
    out_gate,
    beta_logit,
    step_logit,
    conv_weight,
    decay_log,
    decay_bias,
    head_gain,
    lengths,
):
    core_output = mixer(
        mixed_qkv, out_gate, beta_logit, step_logit, conv_weight, decay_log, decay_bias, head_gain, lengths
    )
    normed = normalize_rows(moe_input, moe_gain).astype(jnp.bfloat16)
    if lax.axis_size("expert") * lax.axis_size("fsdp") * expert_gate.shape[0] <= 64:
        moe_output = dense_experts(
            normed, routes, route_gates, expert_gate, expert_up, expert_down,
            shared_gate, shared_up, shared_down, shared_switch,
        )
        return (moe_output, core_output)
    tok_rows, top_count = routes.shape
    features = normed.shape[1]
    expert_count = lax.axis_size("expert")
    dp_count = lax.axis_size("dp")
    local_experts = expert_gate.shape[0]
    send_count = expert_count * dp_count
    all_experts = send_count * local_experts
    capacity = max(2, min(tok_rows, 5 * tok_rows * top_count // (4 * all_experts)))
    flat_routes = routes.reshape(-1)
    route_count = flat_routes.shape[0]
    one_hot = (flat_routes[:, None] == jnp.arange(all_experts, dtype=jnp.int32)[None, :]).astype(
        jnp.int32
    )
    earlier = jnp.cumsum(one_hot, axis=0) - one_hot
    rank_in = jnp.sum(earlier * one_hot, axis=1)
    slot_index = flat_routes * capacity + rank_in
    slot_tokens = (
        jnp.full((all_experts * capacity,), tok_rows, jnp.int32)
        .at[slot_index]
        .set(jnp.arange(route_count, dtype=jnp.int32) // top_count)
    )
    padded_rows = jnp.concatenate([normed, jnp.zeros((1, features), jnp.bfloat16)], axis=0)
    outgoing = padded_rows[slot_tokens]
    full_gate, full_up, full_down, whole_sgate, whole_sup, whole_sdown = (
        lax.all_gather(expert_gate, "fsdp", axis=2, tiled=True),
        lax.all_gather(expert_up, "fsdp", axis=2, tiled=True),
        lax.all_gather(expert_down, "fsdp", axis=1, tiled=True),
        lax.all_gather(shared_gate, "fsdp", axis=1, tiled=True),
        lax.all_gather(shared_up, "fsdp", axis=1, tiled=True),
        lax.all_gather(shared_down, "fsdp", axis=0, tiled=True),
    )
    shared_result = expert_rows(normed, whole_sgate, whole_sup, whole_sdown)
    switch = jax.nn.sigmoid(jnp.dot(normed.astype(jnp.float32), shared_switch, precision=HIGHEST))
    arrived = lax.all_to_all(
        outgoing.reshape(send_count, local_experts, capacity, features),
        ("expert", "dp"),
        split_axis=0,
        concat_axis=0,
        tiled=True,
    )
    gate_part = jnp.einsum("skcd,kdh->skch", arrived, full_gate, preferred_element_type=jnp.float32)
    up_part = jnp.einsum("skcd,kdh->skch", arrived, full_up, preferred_element_type=jnp.float32)
    hidden = (jax.nn.silu(gate_part) * up_part).astype(jnp.bfloat16)
    produced = jnp.einsum(
        "skch,khd->skcd", hidden, full_down, preferred_element_type=jnp.float32
    ).astype(jnp.bfloat16)
    returned = lax.all_to_all(produced, ("expert", "dp"), split_axis=0, concat_axis=0, tiled=True)
    returned = returned.reshape(all_experts * capacity, features)
    picked_rows = returned[slot_index].astype(jnp.float32).reshape(tok_rows, top_count, features)
    routed_sum = jnp.sum(route_gates[:, :, None] * picked_rows, axis=1)
    moe_output = (routed_sum + switch[:, None] * shared_result).astype(jnp.bfloat16)
    return (moe_output, core_output)


def solution(mesh):
    return jax.shard_map(
        local,
        mesh=mesh,
        in_specs=(
            P(("groups", "expert", "fsdp", "dp"), None),
            P(),
            P(("groups", "expert", "fsdp", "dp"), None),
            P(("groups", "expert", "fsdp", "dp"), None),
            P(("expert", "dp"), None, "fsdp"),
            P(("expert", "dp"), None, "fsdp"),
            P(("expert", "dp"), "fsdp", None),
            P(None, "fsdp"),
            P(None, "fsdp"),
            P("fsdp", None),
            P(),
            P(("groups", "expert", "fsdp", "dp"), None, None),
            P(("groups", "expert", "fsdp", "dp"), None, None),
            P(("groups", "expert", "fsdp", "dp"), None, None),
            P(("groups", "expert", "fsdp", "dp"), None, None),
            P(),
            P(),
            P(),
            P(),
            P(("groups", "expert", "fsdp", "dp")),
        ),
        out_specs=(
            P(("groups", "expert", "fsdp", "dp"), None),
            P(("groups", "expert", "fsdp", "dp"), None, None),
        ),
        check_vma=False,
    )
```

```python
import functools
import math

import jax
import jax.numpy as jnp
from jax import lax
from jax.experimental import pallas as pl
from jax.experimental.pallas import tpu as pltpu
from jax.sharding import PartitionSpec as P

EPS = 1e-06
HIGHEST = lax.Precision.HIGHEST


def normalize_rows(rows, gain):
    widened = rows.astype(jnp.float32)
    factor = lax.rsqrt(jnp.mean(widened * widened, axis=-1, keepdims=True) + EPS)
    return widened * factor * gain


def expert_rows(rows, w_gate, w_up, w_down):
    gate_part = jnp.dot(rows, w_gate, preferred_element_type=jnp.float32)
    up_part = jnp.dot(rows, w_up, preferred_element_type=jnp.float32)
    hidden = (jax.nn.silu(gate_part) * up_part).astype(jnp.bfloat16)
    return jnp.dot(hidden, w_down, preferred_element_type=jnp.float32)


def split_bf16(value):
    high = value.astype(jnp.bfloat16)
    low = (value - high.astype(jnp.float32)).astype(jnp.bfloat16)
    return high, low


def product(left, right):
    width = right.shape[1]
    lefts = jnp.concatenate(split_bf16(left), axis=1)
    rights = jnp.concatenate(split_bf16(right), axis=1)
    rights = jnp.concatenate([rights, rights], axis=0)
    both = jnp.dot(lefts, rights, preferred_element_type=jnp.float32)
    return both[:, :width] + both[:, width:]


def product_nt(left, right):
    width = right.shape[0]
    lefts = jnp.concatenate(split_bf16(left), axis=1)
    rights = jnp.concatenate(split_bf16(right), axis=0)
    rights = jnp.concatenate([rights, rights], axis=1)
    both = lax.dot_general(
        lefts, rights, (((1,), (1,)), ((), ())), preferred_element_type=jnp.float32
    )
    return both[:, :width] + both[:, width:]


def sigmoid(value):
    return 1.0 / (1.0 + jnp.exp(-value))


def conv_rows(rows, taps):
    widened = rows.astype(jnp.float32)
    count = taps.shape[0]
    position = lax.broadcasted_iota(jnp.int32, widened.shape, 0)
    total = taps[count - 1 : count, :] * widened
    for back in range(1, count):
        moved = jnp.where(position >= back, pltpu.roll(widened, back, 0), 0.0)
        total = total + taps[count - 1 - back : count - back, :] * moved
    return total * sigmoid(total)


def unit_rows(rows):
    return rows * lax.rsqrt(jnp.sum(rows * rows, axis=-1, keepdims=True) + EPS)


def mixer_prepare(beta_ref, step_ref, log_ref, bias_ref, run_t_ref, run_ref, gate_ref):
    length, heads = step_ref.shape
    row = lax.broadcasted_iota(jnp.int32, (length, length), 0)
    col = lax.broadcasted_iota(jnp.int32, (length, length), 1)
    step = step_ref[...] + bias_ref[...]
    softplus = jnp.maximum(step, 0.0) + jnp.log1p(jnp.exp(-jnp.abs(step)))
    decay = -jnp.exp(log_ref[...]) * softplus
    lower = jnp.where(row >= col, 1.0, 0.0).astype(jnp.bfloat16)
    high, low = split_bf16(decay)
    rest = (decay - high.astype(jnp.float32) - low.astype(jnp.float32)).astype(jnp.bfloat16)
    running = jnp.zeros((length, heads), jnp.float32)
    for piece in (rest, low, high):
        running = running + jnp.dot(lower, piece, preferred_element_type=jnp.float32)
    padded = jnp.concatenate(
        [running, jnp.zeros((length, length - heads), jnp.float32)], axis=1
    )
    run_ref[...] = padded
    run_t_ref[...] = jnp.transpose(padded)
    gate_ref[...] = jnp.concatenate(
        [sigmoid(beta_ref[...]), jnp.zeros((length, length - heads), jnp.float32)], axis=1
    )


def mixer_group(
    group, key_heads, total_heads, repeat, size,
    qkv_ref, gate_in_ref, taps_ref, gain_ref, live, run_t_ref, run_ref, gate_ref, out_ref,
):
    length = qkv_ref.shape[0]
    span = key_heads * size
    wide = span * repeat

    def columns(base, width):
        return pl.ds(pl.multiple_of(base + group * width, size), width)

    row = lax.broadcasted_iota(jnp.int32, (length, length), 0)
    col = lax.broadcasted_iota(jnp.int32, (length, length), 1)
    q_cols = columns(0, span)
    k_cols = columns(total_heads * size, span)
    v_cols = columns(2 * total_heads * size, wide)
    queries = conv_rows(qkv_ref[:, q_cols], taps_ref[:, q_cols])
    keys = conv_rows(qkv_ref[:, k_cols], taps_ref[:, k_cols])
    values = conv_rows(qkv_ref[:, v_cols], taps_ref[:, v_cols])
    running_all, gates_all = run_ref[...], gate_ref[...]
    systems, scores, targets = [], [], []
    for key_head in range(key_heads):
        here = slice(key_head * size, (key_head + 1) * size)
        query = unit_rows(queries[:, here]) * (1.0 / math.sqrt(size))
        key = unit_rows(keys[:, here])
        both = product_nt(jnp.concatenate([query, key], axis=0), key)
        for part in range(repeat):
            local_head = key_head * repeat + part
            head = group * (key_heads * repeat) + local_head
            run_col = jnp.sum(jnp.where(col == head, running_all, 0.0), axis=1, keepdims=True)
            beta = jnp.sum(jnp.where(col == head, gates_all, 0.0), axis=1, keepdims=True)
            run_row = run_t_ref[pl.ds(head, 1), :]
            spread = jnp.where(row >= col, run_col - run_row, 0.0)
            factors = jnp.where(row >= col, jnp.exp(spread), 0.0)
            scores.append(both[:length] * factors)
            systems.append(jnp.where(row > col, beta * both[length:] * factors, 0.0))
            targets.append(beta * values[:, local_head * size : (local_head + 1) * size])
    eye = jnp.where(row == col, 1.0, 0.0)
    block = 8
    near = (row // block) == (col // block)
    firsts = [jnp.where(near, system, 0.0) for system in systems]
    seconds = [product(first, first) for first in firsts]
    fourths = [product(second, second) for second in seconds]
    inverses = [
        eye - first + second - product(first, second) for first, second in zip(firsts, seconds)
    ]
    inverses = [
        inverse + product(inverse, fourth) for inverse, fourth in zip(inverses, fourths)
    ]
    while block < length:
        joined = ((row // (2 * block)) == (col // (2 * block))) & ((row // block) != (col // block))
        links = [jnp.where(joined, system, 0.0) for system in systems]
        halves = [product(link, inverse) for link, inverse in zip(links, inverses)]
        inverses = [
            inverse - product(inverse, half) for inverse, half in zip(inverses, halves)
        ]
        block = 2 * block
    updates = [product(inverse, target) for inverse, target in zip(inverses, targets)]
    results = [product(score, update) for score, update in zip(scores, updates)]
    position = lax.broadcasted_iota(jnp.int32, (length, size), 0)
    for local_head, attended in enumerate(results):
        head = group * (key_heads * repeat) + local_head
        head_cols = pl.ds(pl.multiple_of(head * size, size), size)
        factor = lax.rsqrt(jnp.mean(attended * attended, axis=-1, keepdims=True) + EPS)
        gate = gate_in_ref[:, head_cols].astype(jnp.float32)
        gated = attended * factor * gain_ref[...] * (gate * sigmoid(gate))
        out_ref[:, head_cols] = jnp.where(position < live, gated, 0.0).astype(jnp.bfloat16)


def mixer_kernel(
    key_heads, total_heads, repeat, size,
    live_ref, qkv_ref, gate_in_ref, beta_ref, step_ref, taps_ref, log_ref, bias_ref, gain_ref,
    out_ref, run_t_ref, run_ref, gate_ref,
):
    request = pl.program_id(0)
    mixer_prepare(beta_ref, step_ref, log_ref, bias_ref, run_t_ref, run_ref, gate_ref)

    @pl.loop(0, total_heads // key_heads)
    def _(group):
        mixer_group(
            group, key_heads, total_heads, repeat, size,
            qkv_ref, gate_in_ref, taps_ref, gain_ref, live_ref[request],
            run_t_ref, run_ref, gate_ref, out_ref,
        )


def mixer(
    mixed_qkv, out_gate, beta_logit, step_logit, conv_weight, decay_log, decay_bias, head_gain, lengths
):
    requests, length, channels = mixed_qkv.shape
    heads = decay_log.shape[0]
    size = head_gain.shape[0]
    total_heads = (channels - heads * size) // (2 * size)
    repeat = heads // total_heads

    def whole(array):
        return pl.BlockSpec(array.shape, lambda r: (0,) * array.ndim)

    def one(array):
        return pl.BlockSpec((None,) + array.shape[1:], lambda r: (r, 0, 0))

    small = [conv_weight, decay_log[None, :], decay_bias[None, :], head_gain[None, :]]
    return pl.pallas_call(
        functools.partial(mixer_kernel, 2, total_heads, repeat, size),
        grid=(requests,),
        out_shape=jax.ShapeDtypeStruct(out_gate.shape, jnp.bfloat16),
        in_specs=[pl.BlockSpec(memory_space=pltpu.SMEM)]
        + [one(array) for array in (mixed_qkv, out_gate, beta_logit, step_logit)]
        + [whole(array) for array in small],
        out_specs=one(out_gate),
        scratch_shapes=[pltpu.VMEM((length, length), jnp.float32)] * 3,
        compiler_params=pltpu.CompilerParams(vmem_limit_bytes=32 * 1024 * 1024),
        cost_estimate=pl.CostEstimate(
            flops=20_000_000_000, bytes_accessed=4_000_000, transcendentals=0
        ),
    )(lengths, mixed_qkv, out_gate, beta_logit, step_logit, *small)


MESH = pl.DeviceIdType.MESH


def exchange_kernel(
    top_count,
    input_ref, gain_ref, routes_ref, weights_ref, gate_ref, up_ref, down_ref,
    sgate_ref, sup_ref, sdown_ref, switch_ref,
    out_ref,
    held, other_gate, other_up, other_down, hidden, shared_hidden, kept, staged,
    back_far, back_near, back_line,
    weight_send, weight_recv, line_send, near_send, far_send, held_recv,
    back_line_send, back_near_send, back_far_send,
    back_line_recv, back_near_recv, back_far_recv,
):
    tokens, features = input_ref.shape
    groups, expert = lax.axis_index("groups"), lax.axis_index("expert")
    cross, core = lax.axis_index("fsdp"), lax.axis_index("dp")
    line, side = expert // 2, expert % 2

    def device(line_at, side_at, cross_at, core_at):
        return (groups, line_at * 2 + side_at, cross_at, core_at)

    near = device(line, side + (1 - core) * (1 - 2 * side), cross + core * (1 - 2 * cross), core)
    far = device(line, side + core * (1 - 2 * side), cross + (1 - core) * (1 - 2 * cross), core)
    sibling = device(line, side, cross, 1 - core)
    ahead = [device((line + step) % 4, side, cross, core) for step in range(4)]
    behind = [device((line + 4 - step) % 4, side, cross, core) for step in range(4)]

    lane = lax.broadcasted_iota(jnp.int32, (tokens, 128), 1)
    per_core = gate_ref.shape[0]
    experts = 16 * per_core
    widened = input_ref[...].astype(jnp.float32)
    factor = lax.rsqrt(jnp.mean(widened * widened, axis=-1, keepdims=True) + EPS)
    held[0, :, 0:features] = (widened * factor * gain_ref[...]).astype(jnp.bfloat16)
    share = jnp.zeros((tokens, 128), jnp.float32)
    for choice in range(top_count):
        match = (lane % experts) == routes_ref[:, choice : choice + 1]
        share = share + jnp.where(match, weights_ref[:, choice : choice + 1], 0.0)
    high = share.astype(jnp.bfloat16).astype(jnp.float32)
    held[0, :, features : features + 128] = jnp.where(
        lane < experts, high, share - high
    ).astype(jnp.bfloat16)

    barrier = pltpu.get_barrier_semaphore()
    for partner in (near, far, sibling, ahead[1], ahead[2], ahead[3]):
        pl.semaphore_signal(barrier, inc=1, device_id=partner, device_id_type=MESH)
    pl.semaphore_wait(barrier, 6)

    def send(source, target, send_sem, recv_sem, partner):
        copy = pltpu.make_async_remote_copy(
            src_ref=source, dst_ref=target, send_sem=send_sem, recv_sem=recv_sem,
            device_id=partner, device_id_type=MESH,
        )
        copy.start()
        return copy

    lines, nears, fars = {}, {}, {}

    def send_near(slot):
        nears[slot] = send(
            held.at[slot], held.at[4 + slot], near_send.at[slot], held_recv.at[4 + slot], near
        )

    def send_far(slot):
        fars[slot] = send(
            held.at[slot], held.at[8 + slot], far_send.at[slot], held_recv.at[8 + slot], far
        )

    def arrived(slot):
        if slot < 4:
            lines[slot].wait_recv()
        elif slot < 8:
            nears[slot - 4].wait_recv()
        else:
            fars[slot - 8].wait_recv()

    for step in (2, 1, 3):
        lines[step] = send(
            held.at[0], held.at[step], line_send.at[step], held_recv.at[step], ahead[step]
        )
    send_near(0)
    send_far(0)
    exchanged = [
        send(source, target, weight_send.at[at], weight_recv.at[at], sibling)
        for at, (source, target) in enumerate(
            [(gate_ref, other_gate), (up_ref, other_up), (down_ref, other_down)]
        )
    ]

    def rows_of(slots):
        return jnp.concatenate([held[slot, :, 0:features] for slot in slots], axis=0)

    def share_of(slots, name):
        columns = [
            jnp.sum(
                jnp.where(
                    (lane == name) | (lane == name + experts),
                    held[slot, :, features : features + 128].astype(jnp.float32),
                    0.0,
                ),
                axis=1,
                keepdims=True,
            )
            for slot in slots
        ]
        return jnp.concatenate(columns, axis=0)

    def gated(rows, gate, up, scale):
        gate_part = jnp.dot(rows, gate, preferred_element_type=jnp.float32)
        up_part = jnp.dot(rows, up, preferred_element_type=jnp.float32)
        return (gate_part * sigmoid(gate_part) * up_part * scale).astype(jnp.bfloat16)

    width = gate_ref.shape[2]
    depth = per_core * width

    def experts_on(slots, with_shared):
        first = expert * (2 * per_core)

        @pl.loop(0, per_core)
        def _(index):
            rows = rows_of(slots)
            at = pl.multiple_of(index * width, width)
            hidden[:, pl.ds(at, width)] = gated(
                rows, gate_ref[index], up_ref[index],
                share_of(slots, first + core * per_core + index),
            )
            hidden[:, pl.ds(depth + at, width)] = gated(
                rows, other_gate[index], other_up[index],
                share_of(slots, first + (1 - core) * per_core + index),
            )

        if with_shared:
            scales = []
            for slot, live in zip(slots, (1, core, 1 - core, 0)):
                rows = held[slot, :, 0:features].astype(jnp.float32)
                total = jnp.sum(rows * switch_ref[...], axis=-1, keepdims=True)
                scales.append(sigmoid(total) * (jnp.zeros_like(total) + live))
            shared_hidden[...] = gated(
                rows_of(slots), sgate_ref[...], sup_ref[...], jnp.concatenate(scales, axis=0)
            )

        tile = 256

        @pl.loop(0, features // tile)
        def _(index):
            columns = pl.ds(pl.multiple_of(index * tile, tile), tile)
            total = jnp.dot(
                hidden[:, 0:depth], down_ref[:, columns], preferred_element_type=jnp.float32
            )
            total = total + jnp.dot(
                hidden[:, depth : 2 * depth], other_down[:, columns],
                preferred_element_type=jnp.float32,
            )
            if with_shared:
                total = total + jnp.dot(
                    shared_hidden[...], sdown_ref[:, columns], preferred_element_type=jnp.float32
                )
            for at, slot in enumerate(slots):
                part = total[at * tokens : (at + 1) * tokens]
                if slot < 8:
                    kept[slot, :, columns] = part
                else:
                    staged[slot, :, columns] = part.astype(jnp.bfloat16)

    back_fars, back_nears, back_lines = {}, {}, {}

    def return_far(slot):
        back_fars[slot] = send(
            staged.at[8 + slot], back_far.at[slot], back_far_send.at[slot],
            back_far_recv.at[slot], far,
        )

    def forward(slot):
        arrived(slot)
        send_near(slot)
        send_far(slot)

    arrived(4)
    send_far(4)
    forward(1)
    forward(3)
    for copy in exchanged:
        copy.wait_recv()
    arrived(8)
    arrived(12)
    experts_on((0, 4, 8, 12), True)
    return_far(0)
    return_far(4)
    forward(2)
    for slot in (5, 7, 6):
        arrived(slot)
        send_far(slot)
    experts_on((1, 3, 5, 7), False)
    for slot in (9, 11, 13, 15):
        arrived(slot)
    experts_on((9, 11, 13, 15), False)
    for slot in (5, 7, 1, 3):
        return_far(slot)
    arrived(10)
    arrived(14)
    experts_on((2, 6, 10, 14), False)
    return_far(6)
    return_far(2)

    for slot in (4, 5, 7, 6):
        back_fars[slot].wait_recv()
        staged[slot] = (kept[slot] + back_far[slot].astype(jnp.float32)).astype(jnp.bfloat16)
        back_nears[slot - 4] = send(
            staged.at[slot], back_near.at[slot - 4], back_near_send.at[slot - 4],
            back_near_recv.at[slot - 4], near,
        )
    for slot in (1, 3, 2):
        back_fars[slot].wait_recv()
        back_nears[slot].wait_recv()
        staged[slot] = (
            kept[slot] + back_far[slot].astype(jnp.float32) + back_near[slot].astype(jnp.float32)
        ).astype(jnp.bfloat16)
        back_lines[slot] = send(
            staged.at[slot], back_line.at[slot], back_line_send.at[slot],
            back_line_recv.at[slot], behind[slot],
        )
    back_fars[0].wait_recv()
    back_nears[0].wait_recv()
    total = kept[0] + back_far[0].astype(jnp.float32) + back_near[0].astype(jnp.float32)
    for slot in (1, 3, 2):
        back_lines[slot].wait_recv()
        total = total + back_line[slot].astype(jnp.float32)
    out_ref[...] = total.astype(jnp.bfloat16)
    for copies in (lines, nears, fars, back_fars, back_nears, back_lines):
        for copy in copies.values():
            copy.wait_send()
    for copy in exchanged:
        copy.wait_send()


def exchanged_experts(
    moe_input, moe_gain, routes, route_gates, expert_gate, expert_up, expert_down,
    shared_gate, shared_up, shared_down, shared_switch,
):
    tokens, features = moe_input.shape
    per_core, _, width = expert_gate.shape
    down = expert_down.reshape(per_core * width, features)
    block = (tokens, features)
    bf16, f32, dma = jnp.bfloat16, jnp.float32, pltpu.SemaphoreType.DMA
    return pl.pallas_call(
        functools.partial(exchange_kernel, routes.shape[1]),
        out_shape=jax.ShapeDtypeStruct(block, bf16),
        in_specs=[pl.BlockSpec(memory_space=pltpu.VMEM)] * 11,
        out_specs=pl.BlockSpec(memory_space=pltpu.VMEM),
        scratch_shapes=[
            pltpu.VMEM((16, tokens, features + 128), bf16),
            pltpu.VMEM(expert_gate.shape, bf16),
            pltpu.VMEM(expert_up.shape, bf16),
            pltpu.VMEM(down.shape, bf16),
            pltpu.VMEM((4 * tokens, 2 * per_core * width), bf16),
            pltpu.VMEM((4 * tokens, shared_gate.shape[1]), bf16),
            pltpu.VMEM((8,) + block, f32),
            pltpu.VMEM((16,) + block, bf16),
            pltpu.VMEM((8,) + block, bf16),
            pltpu.VMEM((4,) + block, bf16),
            pltpu.VMEM((4,) + block, bf16),
        ]
        + [dma((count,)) for count in (3, 3, 4, 4, 8, 16, 4, 4, 8, 4, 4, 8)],
        compiler_params=pltpu.CompilerParams(
            collective_id=0, has_side_effects=True, vmem_limit_bytes=56 * 1024 * 1024
        ),
        cost_estimate=pl.CostEstimate(
            flops=13_000_000_000, bytes_accessed=6_000_000, transcendentals=0
        ),
    )(
        moe_input, moe_gain[None, :], routes, route_gates, expert_gate, expert_up, down,
        shared_gate, shared_up, shared_down, shared_switch[None, :],
    )


def local(
    moe_input,
    moe_gain,
    routes,
    route_gates,
    expert_gate,
    expert_up,
    expert_down,
    shared_gate,
    shared_up,
    shared_down,
    shared_switch,
    mixed_qkv,
    out_gate,
    beta_logit,
    step_logit,
    conv_weight,
    decay_log,
    decay_bias,
    head_gain,
    lengths,
):
    core_output = mixer(
        mixed_qkv, out_gate, beta_logit, step_logit, conv_weight, decay_log, decay_bias, head_gain, lengths
    )
    normed = normalize_rows(moe_input, moe_gain).astype(jnp.bfloat16)
    if (lax.axis_size("expert"), lax.axis_size("fsdp"), lax.axis_size("dp")) == (8, 2, 2):
        moe_output = exchanged_experts(
            moe_input, moe_gain, routes, route_gates, expert_gate, expert_up, expert_down,
            shared_gate, shared_up, shared_down, shared_switch,
        )
        return (moe_output, core_output)
    tok_rows, top_count = routes.shape
    features = normed.shape[1]
    expert_count = lax.axis_size("expert")
    dp_count = lax.axis_size("dp")
    local_experts = expert_gate.shape[0]
    send_count = expert_count * dp_count
    all_experts = send_count * local_experts
    capacity = max(2, min(tok_rows, 5 * tok_rows * top_count // (4 * all_experts)))
    flat_routes = routes.reshape(-1)
    route_count = flat_routes.shape[0]
    one_hot = (flat_routes[:, None] == jnp.arange(all_experts, dtype=jnp.int32)[None, :]).astype(
        jnp.int32
    )
    earlier = jnp.cumsum(one_hot, axis=0) - one_hot
    rank_in = jnp.sum(earlier * one_hot, axis=1)
    slot_index = flat_routes * capacity + rank_in
    slot_tokens = (
        jnp.full((all_experts * capacity,), tok_rows, jnp.int32)
        .at[slot_index]
        .set(jnp.arange(route_count, dtype=jnp.int32) // top_count)
    )
    padded_rows = jnp.concatenate([normed, jnp.zeros((1, features), jnp.bfloat16)], axis=0)
    outgoing = padded_rows[slot_tokens]
    full_gate, full_up, full_down, whole_sgate, whole_sup, whole_sdown = (
        lax.all_gather(expert_gate, "fsdp", axis=2, tiled=True),
        lax.all_gather(expert_up, "fsdp", axis=2, tiled=True),
        lax.all_gather(expert_down, "fsdp", axis=1, tiled=True),
        lax.all_gather(shared_gate, "fsdp", axis=1, tiled=True),
        lax.all_gather(shared_up, "fsdp", axis=1, tiled=True),
        lax.all_gather(shared_down, "fsdp", axis=0, tiled=True),
    )
    shared_result = expert_rows(normed, whole_sgate, whole_sup, whole_sdown)
    switch = jax.nn.sigmoid(jnp.dot(normed.astype(jnp.float32), shared_switch, precision=HIGHEST))
    arrived = lax.all_to_all(
        outgoing.reshape(send_count, local_experts, capacity, features),
        ("expert", "dp"),
        split_axis=0,
        concat_axis=0,
        tiled=True,
    )
    gate_part = jnp.einsum("skcd,kdh->skch", arrived, full_gate, preferred_element_type=jnp.float32)
    up_part = jnp.einsum("skcd,kdh->skch", arrived, full_up, preferred_element_type=jnp.float32)
    hidden = (jax.nn.silu(gate_part) * up_part).astype(jnp.bfloat16)
    produced = jnp.einsum(
        "skch,khd->skcd", hidden, full_down, preferred_element_type=jnp.float32
    ).astype(jnp.bfloat16)
    returned = lax.all_to_all(produced, ("expert", "dp"), split_axis=0, concat_axis=0, tiled=True)
    returned = returned.reshape(all_experts * capacity, features)
    picked_rows = returned[slot_index].astype(jnp.float32).reshape(tok_rows, top_count, features)
    routed_sum = jnp.sum(route_gates[:, :, None] * picked_rows, axis=1)
    moe_output = (routed_sum + switch[:, None] * shared_result).astype(jnp.bfloat16)
    return (moe_output, core_output)


def solution(mesh):
    return jax.shard_map(
        local,
        mesh=mesh,
        in_specs=(
            P(("groups", "expert", "fsdp", "dp"), None),
            P(),
            P(("groups", "expert", "fsdp", "dp"), None),
            P(("groups", "expert", "fsdp", "dp"), None),
            P(("expert", "dp"), None, "fsdp"),
            P(("expert", "dp"), None, "fsdp"),
            P(("expert", "dp"), "fsdp", None),
            P(None, "fsdp"),
            P(None, "fsdp"),
            P("fsdp", None),
            P(),
            P(("groups", "expert", "fsdp", "dp"), None, None),
            P(("groups", "expert", "fsdp", "dp"), None, None),
            P(("groups", "expert", "fsdp", "dp"), None, None),
            P(("groups", "expert", "fsdp", "dp"), None, None),
            P(),
            P(),
            P(),
            P(),
            P(("groups", "expert", "fsdp", "dp")),
        ),
        out_specs=(
            P(("groups", "expert", "fsdp", "dp"), None),
            P(("groups", "expert", "fsdp", "dp"), None, None),
        ),
        check_vma=False,
    )
```

```python
import functools
import math

import jax
import jax.numpy as jnp
from jax import lax
from jax.experimental import pallas as pl
from jax.experimental.pallas import tpu as pltpu
from jax.sharding import PartitionSpec as P

EPS = 1e-06
HIGHEST = lax.Precision.HIGHEST


def normalize_rows(rows, gain):
    widened = rows.astype(jnp.float32)
    factor = lax.rsqrt(jnp.mean(widened * widened, axis=-1, keepdims=True) + EPS)
    return widened * factor * gain


def expert_rows(rows, w_gate, w_up, w_down):
    gate_part = jnp.dot(rows, w_gate, preferred_element_type=jnp.float32)
    up_part = jnp.dot(rows, w_up, preferred_element_type=jnp.float32)
    hidden = (jax.nn.silu(gate_part) * up_part).astype(jnp.bfloat16)
    return jnp.dot(hidden, w_down, preferred_element_type=jnp.float32)


def split_bf16(value):
    high = value.astype(jnp.bfloat16)
    low = (value - high.astype(jnp.float32)).astype(jnp.bfloat16)
    return high, low


def product(left, right):
    width = right.shape[1]
    lefts = jnp.concatenate(split_bf16(left), axis=1)
    rights = jnp.concatenate(split_bf16(right), axis=1)
    rights = jnp.concatenate([rights, rights], axis=0)
    both = jnp.dot(lefts, rights, preferred_element_type=jnp.float32)
    return both[:, :width] + both[:, width:]


def product_nt(left, right):
    width = right.shape[0]
    lefts = jnp.concatenate(split_bf16(left), axis=1)
    rights = jnp.concatenate(split_bf16(right), axis=0)
    rights = jnp.concatenate([rights, rights], axis=1)
    both = lax.dot_general(
        lefts, rights, (((1,), (1,)), ((), ())), preferred_element_type=jnp.float32
    )
    return both[:, :width] + both[:, width:]


def sigmoid(value):
    return 1.0 / (1.0 + jnp.exp(-value))


def conv_rows(rows, taps):
    widened = rows.astype(jnp.float32)
    count = taps.shape[0]
    position = lax.broadcasted_iota(jnp.int32, widened.shape, 0)
    total = taps[count - 1 : count, :] * widened
    for back in range(1, count):
        moved = jnp.where(position >= back, pltpu.roll(widened, back, 0), 0.0)
        total = total + taps[count - 1 - back : count - back, :] * moved
    return total * sigmoid(total)


def unit_rows(rows):
    return rows * lax.rsqrt(jnp.sum(rows * rows, axis=-1, keepdims=True) + EPS)


def mixer_prepare(beta_ref, step_ref, log_ref, bias_ref, run_t_ref, run_ref, gate_ref):
    length, heads = step_ref.shape
    row = lax.broadcasted_iota(jnp.int32, (length, length), 0)
    col = lax.broadcasted_iota(jnp.int32, (length, length), 1)
    step = step_ref[...] + bias_ref[...]
    softplus = jnp.maximum(step, 0.0) + jnp.log1p(jnp.exp(-jnp.abs(step)))
    decay = -jnp.exp(log_ref[...]) * softplus
    lower = jnp.where(row >= col, 1.0, 0.0).astype(jnp.bfloat16)
    high, low = split_bf16(decay)
    rest = (decay - high.astype(jnp.float32) - low.astype(jnp.float32)).astype(jnp.bfloat16)
    running = jnp.zeros((length, heads), jnp.float32)
    for piece in (rest, low, high):
        running = running + jnp.dot(lower, piece, preferred_element_type=jnp.float32)
    padded = jnp.concatenate(
        [running, jnp.zeros((length, length - heads), jnp.float32)], axis=1
    )
    run_ref[...] = padded
    run_t_ref[...] = jnp.transpose(padded)
    gate_ref[...] = jnp.concatenate(
        [sigmoid(beta_ref[...]), jnp.zeros((length, length - heads), jnp.float32)], axis=1
    )


def mixer_group(
    group, key_heads, total_heads, repeat, size,
    qkv_ref, gate_in_ref, taps_ref, gain_ref, live, run_t_ref, run_ref, gate_ref, out_ref,
):
    length = qkv_ref.shape[0]
    span = key_heads * size
    wide = span * repeat

    def columns(base, width):
        return pl.ds(pl.multiple_of(base + group * width, size), width)

    row = lax.broadcasted_iota(jnp.int32, (length, length), 0)
    col = lax.broadcasted_iota(jnp.int32, (length, length), 1)
    q_cols = columns(0, span)
    k_cols = columns(total_heads * size, span)
    v_cols = columns(2 * total_heads * size, wide)
    queries = conv_rows(qkv_ref[:, q_cols], taps_ref[:, q_cols])
    keys = conv_rows(qkv_ref[:, k_cols], taps_ref[:, k_cols])
    values = conv_rows(qkv_ref[:, v_cols], taps_ref[:, v_cols])
    running_all, gates_all = run_ref[...], gate_ref[...]
    systems, scores, targets = [], [], []
    for key_head in range(key_heads):
        here = slice(key_head * size, (key_head + 1) * size)
        query = unit_rows(queries[:, here]) * (1.0 / math.sqrt(size))
        key = unit_rows(keys[:, here])
        both = product_nt(jnp.concatenate([query, key], axis=0), key)
        for part in range(repeat):
            local_head = key_head * repeat + part
            head = group * (key_heads * repeat) + local_head
            run_col = jnp.sum(jnp.where(col == head, running_all, 0.0), axis=1, keepdims=True)
            beta = jnp.sum(jnp.where(col == head, gates_all, 0.0), axis=1, keepdims=True)
            run_row = run_t_ref[pl.ds(head, 1), :]
            spread = jnp.where(row >= col, run_col - run_row, 0.0)
            factors = jnp.where(row >= col, jnp.exp(spread), 0.0)
            scores.append(both[:length] * factors)
            systems.append(jnp.where(row > col, beta * both[length:] * factors, 0.0))
            targets.append(beta * values[:, local_head * size : (local_head + 1) * size])
    eye = jnp.where(row == col, 1.0, 0.0)
    block = 8
    near = (row // block) == (col // block)
    firsts = [jnp.where(near, system, 0.0) for system in systems]
    seconds = [product(first, first) for first in firsts]
    fourths = [product(second, second) for second in seconds]
    inverses = [
        eye - first + second - product(first, second) for first, second in zip(firsts, seconds)
    ]
    inverses = [
        inverse + product(inverse, fourth) for inverse, fourth in zip(inverses, fourths)
    ]
    while block < length:
        joined = ((row // (2 * block)) == (col // (2 * block))) & ((row // block) != (col // block))
        links = [jnp.where(joined, system, 0.0) for system in systems]
        halves = [product(link, inverse) for link, inverse in zip(links, inverses)]
        inverses = [
            inverse - product(inverse, half) for inverse, half in zip(inverses, halves)
        ]
        block = 2 * block
    updates = [product(inverse, target) for inverse, target in zip(inverses, targets)]
    results = [product(score, update) for score, update in zip(scores, updates)]
    position = lax.broadcasted_iota(jnp.int32, (length, size), 0)
    for local_head, attended in enumerate(results):
        head = group * (key_heads * repeat) + local_head
        head_cols = pl.ds(pl.multiple_of(head * size, size), size)
        factor = lax.rsqrt(jnp.mean(attended * attended, axis=-1, keepdims=True) + EPS)
        gate = gate_in_ref[:, head_cols].astype(jnp.float32)
        gated = attended * factor * gain_ref[...] * (gate * sigmoid(gate))
        out_ref[:, head_cols] = jnp.where(position < live, gated, 0.0).astype(jnp.bfloat16)


def mixer_kernel(
    key_heads, total_heads, repeat, size,
    live_ref, qkv_ref, gate_in_ref, beta_ref, step_ref, taps_ref, log_ref, bias_ref, gain_ref,
    out_ref, run_t_ref, run_ref, gate_ref,
):
    request = pl.program_id(0)
    mixer_prepare(beta_ref, step_ref, log_ref, bias_ref, run_t_ref, run_ref, gate_ref)

    @pl.loop(0, total_heads // key_heads)
    def _(group):
        mixer_group(
            group, key_heads, total_heads, repeat, size,
            qkv_ref, gate_in_ref, taps_ref, gain_ref, live_ref[request],
            run_t_ref, run_ref, gate_ref, out_ref,
        )


def mixer(
    mixed_qkv, out_gate, beta_logit, step_logit, conv_weight, decay_log, decay_bias, head_gain, lengths
):
    requests, length, channels = mixed_qkv.shape
    heads = decay_log.shape[0]
    size = head_gain.shape[0]
    total_heads = (channels - heads * size) // (2 * size)
    repeat = heads // total_heads

    def whole(array):
        return pl.BlockSpec(array.shape, lambda r: (0,) * array.ndim)

    def one(array):
        return pl.BlockSpec((None,) + array.shape[1:], lambda r: (r, 0, 0))

    small = [conv_weight, decay_log[None, :], decay_bias[None, :], head_gain[None, :]]
    return pl.pallas_call(
        functools.partial(mixer_kernel, 2, total_heads, repeat, size),
        grid=(requests,),
        out_shape=jax.ShapeDtypeStruct(out_gate.shape, jnp.bfloat16),
        in_specs=[pl.BlockSpec(memory_space=pltpu.SMEM)]
        + [one(array) for array in (mixed_qkv, out_gate, beta_logit, step_logit)]
        + [whole(array) for array in small],
        out_specs=one(out_gate),
        scratch_shapes=[pltpu.VMEM((length, length), jnp.float32)] * 3,
        compiler_params=pltpu.CompilerParams(vmem_limit_bytes=32 * 1024 * 1024),
        cost_estimate=pl.CostEstimate(
            flops=20_000_000_000, bytes_accessed=4_000_000, transcendentals=0
        ),
    )(lengths, mixed_qkv, out_gate, beta_logit, step_logit, *small)


MESH = pl.DeviceIdType.MESH


def exchange_kernel(
    top_count, mixer_heads,
    input_ref, gain_ref, routes_ref, weights_ref, gate_ref, up_ref, down_ref,
    sgate_ref, sup_ref, sdown_ref, switch_ref,
    live_ref, qkv_ref, gate_in_ref, beta_ref, step_ref, taps_ref, log_ref, bias_ref, head_gain_ref,
    out_ref, core_ref,
    held, other_gate, other_up, other_down, hidden, shared_hidden, kept, staged,
    back_far, back_near, back_line,
    weight_send, weight_recv, line_send, near_send, far_send, held_recv,
    back_line_send, back_near_send, back_far_send,
    back_line_recv, back_near_recv, back_far_recv,
    run_t_ref, run_ref, strength_ref,
):
    tokens, features = input_ref.shape
    groups, expert = lax.axis_index("groups"), lax.axis_index("expert")
    cross, core = lax.axis_index("fsdp"), lax.axis_index("dp")
    line, side = expert // 2, expert % 2

    def device(line_at, side_at, cross_at, core_at):
        return (groups, line_at * 2 + side_at, cross_at, core_at)

    near = device(line, side + (1 - core) * (1 - 2 * side), cross + core * (1 - 2 * cross), core)
    far = device(line, side + core * (1 - 2 * side), cross + (1 - core) * (1 - 2 * cross), core)
    sibling = device(line, side, cross, 1 - core)
    places = (line, line + 1 - 2 * (line % 2), (line + 2) % 4, 3 - line)
    paired = [device(place, side, cross, core) for place in places]

    lane = lax.broadcasted_iota(jnp.int32, (tokens, 128), 1)
    per_core = gate_ref.shape[0]
    experts = 16 * per_core
    widened = input_ref[...].astype(jnp.float32)
    factor = lax.rsqrt(jnp.mean(widened * widened, axis=-1, keepdims=True) + EPS)
    held[0, :, 0:features] = (widened * factor * gain_ref[...]).astype(jnp.bfloat16)
    share = jnp.zeros((tokens, 128), jnp.float32)
    for choice in range(top_count):
        match = (lane % experts) == routes_ref[:, choice : choice + 1]
        share = share + jnp.where(match, weights_ref[:, choice : choice + 1], 0.0)
    high = share.astype(jnp.bfloat16).astype(jnp.float32)
    held[0, :, features : features + 128] = jnp.where(
        lane < experts, high, share - high
    ).astype(jnp.bfloat16)

    barrier = pltpu.get_barrier_semaphore()
    for partner in (near, far, sibling, paired[1], paired[2], paired[3]):
        pl.semaphore_signal(barrier, inc=1, device_id=partner, device_id_type=MESH)
    pl.semaphore_wait(barrier, 6)

    def send(source, target, send_sem, recv_sem, partner):
        copy = pltpu.make_async_remote_copy(
            src_ref=source, dst_ref=target, send_sem=send_sem, recv_sem=recv_sem,
            device_id=partner, device_id_type=MESH,
        )
        copy.start()
        return copy

    lines, nears, fars = {}, {}, {}

    def send_near(slot):
        nears[slot] = send(
            held.at[slot], held.at[4 + slot], near_send.at[slot], held_recv.at[4 + slot], near
        )

    def send_far(slot):
        fars[slot] = send(
            held.at[slot], held.at[8 + slot], far_send.at[slot], held_recv.at[8 + slot], far
        )

    def arrived(slot):
        if slot < 4:
            lines[slot].wait_recv()
        elif slot < 8:
            nears[slot - 4].wait_recv()
        else:
            fars[slot - 8].wait_recv()

    for step in (1, 3, 2):
        lines[step] = send(
            held.at[0], held.at[step], line_send.at[step], held_recv.at[step], paired[step]
        )
    send_near(0)
    send_far(0)
    exchanged = [
        send(source, target, weight_send.at[at], weight_recv.at[at], sibling)
        for at, (source, target) in enumerate(
            [(gate_ref, other_gate), (up_ref, other_up), (down_ref, other_down)]
        )
    ]

    def rows_of(slots):
        return jnp.concatenate([held[slot, :, 0:features] for slot in slots], axis=0)

    def share_of(slots, name):
        columns = [
            jnp.sum(
                jnp.where(
                    (lane == name) | (lane == name + experts),
                    held[slot, :, features : features + 128].astype(jnp.float32),
                    0.0,
                ),
                axis=1,
                keepdims=True,
            )
            for slot in slots
        ]
        return jnp.concatenate(columns, axis=0)

    def gated(rows, gate, up, scale):
        gate_part = jnp.dot(rows, gate, preferred_element_type=jnp.float32)
        up_part = jnp.dot(rows, up, preferred_element_type=jnp.float32)
        return (gate_part * sigmoid(gate_part) * up_part * scale).astype(jnp.bfloat16)

    width = gate_ref.shape[2]
    depth = per_core * width

    def experts_on(slots, with_shared):
        first = expert * (2 * per_core)

        @pl.loop(0, per_core)
        def _(index):
            rows = rows_of(slots)
            at = pl.multiple_of(index * width, width)
            hidden[:, pl.ds(at, width)] = gated(
                rows, gate_ref[index], up_ref[index],
                share_of(slots, first + core * per_core + index),
            )
            hidden[:, pl.ds(depth + at, width)] = gated(
                rows, other_gate[index], other_up[index],
                share_of(slots, first + (1 - core) * per_core + index),
            )

        if with_shared:
            scales = []
            for slot, live in zip(slots, (1, core, 1 - core, 0)):
                rows = held[slot, :, 0:features].astype(jnp.float32)
                total = jnp.sum(rows * switch_ref[...], axis=-1, keepdims=True)
                scales.append(sigmoid(total) * (jnp.zeros_like(total) + live))
            shared_hidden[...] = gated(
                rows_of(slots), sgate_ref[...], sup_ref[...], jnp.concatenate(scales, axis=0)
            )

        tile = 256

        @pl.loop(0, features // tile)
        def _(index):
            columns = pl.ds(pl.multiple_of(index * tile, tile), tile)
            total = jnp.dot(
                hidden[:, 0:depth], down_ref[:, columns], preferred_element_type=jnp.float32
            )
            total = total + jnp.dot(
                hidden[:, depth : 2 * depth], other_down[:, columns],
                preferred_element_type=jnp.float32,
            )
            if with_shared:
                total = total + jnp.dot(
                    shared_hidden[...], sdown_ref[:, columns], preferred_element_type=jnp.float32
                )
            for at, slot in enumerate(slots):
                part = total[at * tokens : (at + 1) * tokens]
                if slot < 8:
                    kept[slot, :, columns] = part
                else:
                    staged[slot, :, columns] = part.astype(jnp.bfloat16)

    back_fars, back_nears, back_lines = {}, {}, {}

    def return_far(slot):
        back_fars[slot] = send(
            staged.at[8 + slot], back_far.at[slot], back_far_send.at[slot],
            back_far_recv.at[slot], far,
        )

    def forward(slot):
        arrived(slot)
        send_near(slot)
        send_far(slot)

    def gather_near(slot):
        arrived(4 + slot)
        send_far(4 + slot)

    def run(slot):
        arrived(8 + slot)
        arrived(12 + slot)
        experts_on((slot, 4 + slot, 8 + slot, 12 + slot), slot == 0)
        return_far(4 + slot)
        return_far(slot)

    def reduce_near(slot):
        back_fars[4 + slot].wait_recv()
        staged[4 + slot] = (
            kept[4 + slot] + back_far[4 + slot].astype(jnp.float32)
        ).astype(jnp.bfloat16)
        back_nears[slot] = send(
            staged.at[4 + slot], back_near.at[slot], back_near_send.at[slot],
            back_near_recv.at[slot], near,
        )

    def reduce_line(slot):
        back_fars[slot].wait_recv()
        back_nears[slot].wait_recv()
        staged[slot] = (
            kept[slot] + back_far[slot].astype(jnp.float32) + back_near[slot].astype(jnp.float32)
        ).astype(jnp.bfloat16)
        back_lines[slot] = send(
            staged.at[slot], back_line.at[slot], back_line_send.at[slot],
            back_line_recv.at[slot], paired[slot],
        )

    def mix(start, stop):
        @pl.loop(start, stop)
        def _(group):
            mixer_group(
                group, 2, mixer_heads[0], mixer_heads[1], mixer_heads[2],
                qkv_ref, gate_in_ref, taps_ref, head_gain_ref, live_ref[0],
                run_t_ref, run_ref, strength_ref, core_ref,
            )

    mixer_prepare(beta_ref, step_ref, log_ref, bias_ref, run_t_ref, run_ref, strength_ref)
    gather_near(0)
    forward(1)
    mix(0, 1)
    gather_near(1)
    for copy in exchanged:
        copy.wait_recv()
    run(0)
    forward(3)
    mix(1, 2)
    gather_near(3)
    run(1)
    forward(2)
    reduce_near(0)
    gather_near(2)
    mix(2, 3)
    reduce_near(1)
    run(3)
    reduce_line(1)
    mix(3, mixer_heads[0] // 2)
    run(2)
    reduce_near(3)
    reduce_line(3)
    reduce_near(2)
    reduce_line(2)
    back_fars[0].wait_recv()
    back_nears[0].wait_recv()
    total = kept[0] + back_far[0].astype(jnp.float32) + back_near[0].astype(jnp.float32)
    for slot in (1, 3, 2):
        back_lines[slot].wait_recv()
        total = total + back_line[slot].astype(jnp.float32)
    out_ref[...] = total.astype(jnp.bfloat16)
    for copies in (lines, nears, fars, back_fars, back_nears, back_lines):
        for copy in copies.values():
            copy.wait_send()
    for copy in exchanged:
        copy.wait_send()


def exchanged_experts(
    moe_input, moe_gain, routes, route_gates, expert_gate, expert_up, expert_down,
    shared_gate, shared_up, shared_down, shared_switch,
    mixed_qkv, out_gate, beta_logit, step_logit, conv_weight, decay_log, decay_bias, head_gain, lengths,
):
    tokens, features = moe_input.shape
    _, length, channels = mixed_qkv.shape
    size = head_gain.shape[0]
    heads = decay_log.shape[0]
    key_heads = (channels - heads * size) // (2 * size)
    mixer_heads = (key_heads, heads // key_heads, size)
    vmem = pl.BlockSpec(memory_space=pltpu.VMEM)
    per_core, _, width = expert_gate.shape
    down = expert_down.reshape(per_core * width, features)
    block = (tokens, features)
    bf16, f32, dma = jnp.bfloat16, jnp.float32, pltpu.SemaphoreType.DMA
    moe_output, core_output = pl.pallas_call(
        functools.partial(exchange_kernel, routes.shape[1], mixer_heads),
        out_shape=[jax.ShapeDtypeStruct(block, bf16), jax.ShapeDtypeStruct(out_gate.shape[1:], bf16)],
        in_specs=[vmem] * 11 + [pl.BlockSpec(memory_space=pltpu.SMEM)] + [vmem] * 8,
        out_specs=[vmem, vmem],
        scratch_shapes=[
            pltpu.VMEM((16, tokens, features + 128), bf16),
            pltpu.VMEM(expert_gate.shape, bf16),
            pltpu.VMEM(expert_up.shape, bf16),
            pltpu.VMEM(down.shape, bf16),
            pltpu.VMEM((4 * tokens, 2 * per_core * width), bf16),
            pltpu.VMEM((4 * tokens, shared_gate.shape[1]), bf16),
            pltpu.VMEM((8,) + block, f32),
            pltpu.VMEM((16,) + block, bf16),
            pltpu.VMEM((8,) + block, bf16),
            pltpu.VMEM((4,) + block, bf16),
            pltpu.VMEM((4,) + block, bf16),
        ]
        + [dma((count,)) for count in (3, 3, 4, 4, 8, 16, 4, 4, 8, 4, 4, 8)]
        + [pltpu.VMEM((length, length), f32)] * 3,
        compiler_params=pltpu.CompilerParams(
            collective_id=0, has_side_effects=True, vmem_limit_bytes=56 * 1024 * 1024
        ),
        cost_estimate=pl.CostEstimate(
            flops=13_000_000_000, bytes_accessed=6_000_000, transcendentals=0
        ),
    )(
        moe_input, moe_gain[None, :], routes, route_gates, expert_gate, expert_up, down,
        shared_gate, shared_up, shared_down, shared_switch[None, :],
        lengths, mixed_qkv[0], out_gate[0], beta_logit[0], step_logit[0],
        conv_weight, decay_log[None, :], decay_bias[None, :], head_gain[None, :],
    )
    return moe_output, core_output[None]


def local(
    moe_input,
    moe_gain,
    routes,
    route_gates,
    expert_gate,
    expert_up,
    expert_down,
    shared_gate,
    shared_up,
    shared_down,
    shared_switch,
    mixed_qkv,
    out_gate,
    beta_logit,
    step_logit,
    conv_weight,
    decay_log,
    decay_bias,
    head_gain,
    lengths,
):
    sizes = (lax.axis_size("expert"), lax.axis_size("fsdp"), lax.axis_size("dp"))
    if sizes == (8, 2, 2) and mixed_qkv.shape[0] == 1:
        return exchanged_experts(
            moe_input, moe_gain, routes, route_gates, expert_gate, expert_up, expert_down,
            shared_gate, shared_up, shared_down, shared_switch,
            mixed_qkv, out_gate, beta_logit, step_logit, conv_weight, decay_log, decay_bias, head_gain, lengths,
        )
    core_output = mixer(
        mixed_qkv, out_gate, beta_logit, step_logit, conv_weight, decay_log, decay_bias, head_gain, lengths
    )
    normed = normalize_rows(moe_input, moe_gain).astype(jnp.bfloat16)
    tok_rows, top_count = routes.shape
    features = normed.shape[1]
    expert_count = lax.axis_size("expert")
    dp_count = lax.axis_size("dp")
    local_experts = expert_gate.shape[0]
    send_count = expert_count * dp_count
    all_experts = send_count * local_experts
    capacity = max(2, min(tok_rows, 5 * tok_rows * top_count // (4 * all_experts)))
    flat_routes = routes.reshape(-1)
    route_count = flat_routes.shape[0]
    one_hot = (flat_routes[:, None] == jnp.arange(all_experts, dtype=jnp.int32)[None, :]).astype(
        jnp.int32
    )
    earlier = jnp.cumsum(one_hot, axis=0) - one_hot
    rank_in = jnp.sum(earlier * one_hot, axis=1)
    slot_index = flat_routes * capacity + rank_in
    slot_tokens = (
        jnp.full((all_experts * capacity,), tok_rows, jnp.int32)
        .at[slot_index]
        .set(jnp.arange(route_count, dtype=jnp.int32) // top_count)
    )
    padded_rows = jnp.concatenate([normed, jnp.zeros((1, features), jnp.bfloat16)], axis=0)
    outgoing = padded_rows[slot_tokens]
    full_gate, full_up, full_down, whole_sgate, whole_sup, whole_sdown = (
        lax.all_gather(expert_gate, "fsdp", axis=2, tiled=True),
        lax.all_gather(expert_up, "fsdp", axis=2, tiled=True),
        lax.all_gather(expert_down, "fsdp", axis=1, tiled=True),
        lax.all_gather(shared_gate, "fsdp", axis=1, tiled=True),
        lax.all_gather(shared_up, "fsdp", axis=1, tiled=True),
        lax.all_gather(shared_down, "fsdp", axis=0, tiled=True),
    )
    shared_result = expert_rows(normed, whole_sgate, whole_sup, whole_sdown)
    switch = jax.nn.sigmoid(jnp.dot(normed.astype(jnp.float32), shared_switch, precision=HIGHEST))
    arrived = lax.all_to_all(
        outgoing.reshape(send_count, local_experts, capacity, features),
        ("expert", "dp"),
        split_axis=0,
        concat_axis=0,
        tiled=True,
    )
    gate_part = jnp.einsum("skcd,kdh->skch", arrived, full_gate, preferred_element_type=jnp.float32)
    up_part = jnp.einsum("skcd,kdh->skch", arrived, full_up, preferred_element_type=jnp.float32)
    hidden = (jax.nn.silu(gate_part) * up_part).astype(jnp.bfloat16)
    produced = jnp.einsum(
        "skch,khd->skcd", hidden, full_down, preferred_element_type=jnp.float32
    ).astype(jnp.bfloat16)
    returned = lax.all_to_all(produced, ("expert", "dp"), split_axis=0, concat_axis=0, tiled=True)
    returned = returned.reshape(all_experts * capacity, features)
    picked_rows = returned[slot_index].astype(jnp.float32).reshape(tok_rows, top_count, features)
    routed_sum = jnp.sum(route_gates[:, :, None] * picked_rows, axis=1)
    moe_output = (routed_sum + switch[:, None] * shared_result).astype(jnp.bfloat16)
    return (moe_output, core_output)


def solution(mesh):
    return jax.shard_map(
        local,
        mesh=mesh,
        in_specs=(
            P(("groups", "expert", "fsdp", "dp"), None),
            P(),
            P(("groups", "expert", "fsdp", "dp"), None),
            P(("groups", "expert", "fsdp", "dp"), None),
            P(("expert", "dp"), None, "fsdp"),
            P(("expert", "dp"), None, "fsdp"),
            P(("expert", "dp"), "fsdp", None),
            P(None, "fsdp"),
            P(None, "fsdp"),
            P("fsdp", None),
            P(),
            P(("groups", "expert", "fsdp", "dp"), None, None),
            P(("groups", "expert", "fsdp", "dp"), None, None),
            P(("groups", "expert", "fsdp", "dp"), None, None),
            P(("groups", "expert", "fsdp", "dp"), None, None),
            P(),
            P(),
            P(),
            P(),
            P(("groups", "expert", "fsdp", "dp")),
        ),
        out_specs=(
            P(("groups", "expert", "fsdp", "dp"), None),
            P(("groups", "expert", "fsdp", "dp"), None, None),
        ),
        check_vma=False,
    )
```

```python
import functools
import math

import jax
import jax.numpy as jnp
from jax import lax
from jax.experimental import pallas as pl
from jax.experimental.pallas import tpu as pltpu
from jax.sharding import PartitionSpec as P

EPS = 1e-06
HIGHEST = lax.Precision.HIGHEST


def normalize_rows(rows, gain):
    widened = rows.astype(jnp.float32)
    factor = lax.rsqrt(jnp.mean(widened * widened, axis=-1, keepdims=True) + EPS)
    return widened * factor * gain


def expert_rows(rows, w_gate, w_up, w_down):
    gate_part = jnp.dot(rows, w_gate, preferred_element_type=jnp.float32)
    up_part = jnp.dot(rows, w_up, preferred_element_type=jnp.float32)
    hidden = (jax.nn.silu(gate_part) * up_part).astype(jnp.bfloat16)
    return jnp.dot(hidden, w_down, preferred_element_type=jnp.float32)


def split_bf16(value):
    high = value.astype(jnp.bfloat16)
    low = (value - high.astype(jnp.float32)).astype(jnp.bfloat16)
    return high, low


def product(left, right):
    width = right.shape[1]
    lefts = jnp.concatenate(split_bf16(left), axis=1)
    rights = jnp.concatenate(split_bf16(right), axis=1)
    rights = jnp.concatenate([rights, rights], axis=0)
    both = jnp.dot(lefts, rights, preferred_element_type=jnp.float32)
    return both[:, :width] + both[:, width:]


def product_nt(left, right):
    width = right.shape[0]
    lefts = jnp.concatenate(split_bf16(left), axis=1)
    rights = jnp.concatenate(split_bf16(right), axis=0)
    rights = jnp.concatenate([rights, rights], axis=1)
    both = lax.dot_general(
        lefts, rights, (((1,), (1,)), ((), ())), preferred_element_type=jnp.float32
    )
    return both[:, :width] + both[:, width:]


def sigmoid(value):
    return 1.0 / (1.0 + jnp.exp(-value))


def conv_rows(rows, taps):
    widened = rows.astype(jnp.float32)
    count = taps.shape[0]
    position = lax.broadcasted_iota(jnp.int32, widened.shape, 0)
    total = taps[count - 1 : count, :] * widened
    for back in range(1, count):
        moved = jnp.where(position >= back, pltpu.roll(widened, back, 0), 0.0)
        total = total + taps[count - 1 - back : count - back, :] * moved
    return total * sigmoid(total)


def unit_rows(rows):
    return rows * lax.rsqrt(jnp.sum(rows * rows, axis=-1, keepdims=True) + EPS)


def mixer_prepare(beta_ref, step_ref, log_ref, bias_ref, run_t_ref, run_ref, gate_ref):
    length, heads = step_ref.shape
    row = lax.broadcasted_iota(jnp.int32, (length, length), 0)
    col = lax.broadcasted_iota(jnp.int32, (length, length), 1)
    step = step_ref[...] + bias_ref[...]
    softplus = jnp.maximum(step, 0.0) + jnp.log1p(jnp.exp(-jnp.abs(step)))
    decay = -jnp.exp(log_ref[...]) * softplus
    lower = jnp.where(row >= col, 1.0, 0.0).astype(jnp.bfloat16)
    high, low = split_bf16(decay)
    rest = (decay - high.astype(jnp.float32) - low.astype(jnp.float32)).astype(jnp.bfloat16)
    running = jnp.zeros((length, heads), jnp.float32)
    for piece in (rest, low, high):
        running = running + jnp.dot(lower, piece, preferred_element_type=jnp.float32)
    padded = jnp.concatenate(
        [running, jnp.zeros((length, length - heads), jnp.float32)], axis=1
    )
    run_ref[...] = padded
    run_t_ref[...] = jnp.transpose(padded)
    gate_ref[...] = jnp.concatenate(
        [sigmoid(beta_ref[...]), jnp.zeros((length, length - heads), jnp.float32)], axis=1
    )


def mixer_group(
    group, key_heads, total_heads, repeat, size,
    qkv_ref, gate_in_ref, taps_ref, gain_ref, live, run_t_ref, run_ref, gate_ref, out_ref,
):
    length = qkv_ref.shape[0]
    span = key_heads * size
    wide = span * repeat

    def columns(base, width):
        return pl.ds(pl.multiple_of(base + group * width, size), width)

    row = lax.broadcasted_iota(jnp.int32, (length, length), 0)
    col = lax.broadcasted_iota(jnp.int32, (length, length), 1)
    q_cols = columns(0, span)
    k_cols = columns(total_heads * size, span)
    v_cols = columns(2 * total_heads * size, wide)
    queries = conv_rows(qkv_ref[:, q_cols], taps_ref[:, q_cols])
    keys = conv_rows(qkv_ref[:, k_cols], taps_ref[:, k_cols])
    values = conv_rows(qkv_ref[:, v_cols], taps_ref[:, v_cols])
    running_all, gates_all = run_ref[...], gate_ref[...]
    systems, scores, targets = [], [], []
    for key_head in range(key_heads):
        here = slice(key_head * size, (key_head + 1) * size)
        query = unit_rows(queries[:, here]) * (1.0 / math.sqrt(size))
        key = unit_rows(keys[:, here])
        both = product_nt(jnp.concatenate([query, key], axis=0), key)
        for part in range(repeat):
            local_head = key_head * repeat + part
            head = group * (key_heads * repeat) + local_head
            run_col = jnp.sum(jnp.where(col == head, running_all, 0.0), axis=1, keepdims=True)
            beta = jnp.sum(jnp.where(col == head, gates_all, 0.0), axis=1, keepdims=True)
            run_row = run_t_ref[pl.ds(head, 1), :]
            spread = jnp.where(row >= col, run_col - run_row, 0.0)
            factors = jnp.where(row >= col, jnp.exp(spread), 0.0)
            scores.append(both[:length] * factors)
            systems.append(jnp.where(row > col, beta * both[length:] * factors, 0.0))
            targets.append(beta * values[:, local_head * size : (local_head + 1) * size])
    eye = jnp.where(row == col, 1.0, 0.0)
    block = 8
    near = (row // block) == (col // block)
    firsts = [jnp.where(near, system, 0.0) for system in systems]
    seconds = [product(first, first) for first in firsts]
    fourths = [product(second, second) for second in seconds]
    inverses = [
        eye - first + second - product(first, second) for first, second in zip(firsts, seconds)
    ]
    inverses = [
        inverse + product(inverse, fourth) for inverse, fourth in zip(inverses, fourths)
    ]
    while block < length:
        joined = ((row // (2 * block)) == (col // (2 * block))) & ((row // block) != (col // block))
        links = [jnp.where(joined, system, 0.0) for system in systems]
        halves = [product(link, inverse) for link, inverse in zip(links, inverses)]
        inverses = [
            inverse - product(inverse, half) for inverse, half in zip(inverses, halves)
        ]
        block = 2 * block
    updates = [product(inverse, target) for inverse, target in zip(inverses, targets)]
    results = [product(score, update) for score, update in zip(scores, updates)]
    position = lax.broadcasted_iota(jnp.int32, (length, size), 0)
    for local_head, attended in enumerate(results):
        head = group * (key_heads * repeat) + local_head
        head_cols = pl.ds(pl.multiple_of(head * size, size), size)
        factor = lax.rsqrt(jnp.mean(attended * attended, axis=-1, keepdims=True) + EPS)
        gate = gate_in_ref[:, head_cols].astype(jnp.float32)
        gated = attended * factor * gain_ref[...] * (gate * sigmoid(gate))
        out_ref[:, head_cols] = jnp.where(position < live, gated, 0.0).astype(jnp.bfloat16)


def mixer_kernel(
    key_heads, total_heads, repeat, size,
    live_ref, qkv_ref, gate_in_ref, beta_ref, step_ref, taps_ref, log_ref, bias_ref, gain_ref,
    out_ref, run_t_ref, run_ref, gate_ref,
):
    request = pl.program_id(0)
    mixer_prepare(beta_ref, step_ref, log_ref, bias_ref, run_t_ref, run_ref, gate_ref)

    @pl.loop(0, total_heads // key_heads)
    def _(group):
        mixer_group(
            group, key_heads, total_heads, repeat, size,
            qkv_ref, gate_in_ref, taps_ref, gain_ref, live_ref[request],
            run_t_ref, run_ref, gate_ref, out_ref,
        )


def mixer(
    mixed_qkv, out_gate, beta_logit, step_logit, conv_weight, decay_log, decay_bias, head_gain, lengths
):
    requests, length, channels = mixed_qkv.shape
    heads = decay_log.shape[0]
    size = head_gain.shape[0]
    total_heads = (channels - heads * size) // (2 * size)
    repeat = heads // total_heads

    def whole(array):
        return pl.BlockSpec(array.shape, lambda r: (0,) * array.ndim)

    def one(array):
        return pl.BlockSpec((None,) + array.shape[1:], lambda r: (r, 0, 0))

    small = [conv_weight, decay_log[None, :], decay_bias[None, :], head_gain[None, :]]
    return pl.pallas_call(
        functools.partial(mixer_kernel, 2, total_heads, repeat, size),
        grid=(requests,),
        out_shape=jax.ShapeDtypeStruct(out_gate.shape, jnp.bfloat16),
        in_specs=[pl.BlockSpec(memory_space=pltpu.SMEM)]
        + [one(array) for array in (mixed_qkv, out_gate, beta_logit, step_logit)]
        + [whole(array) for array in small],
        out_specs=one(out_gate),
        scratch_shapes=[pltpu.VMEM((length, length), jnp.float32)] * 3,
        compiler_params=pltpu.CompilerParams(vmem_limit_bytes=32 * 1024 * 1024),
        cost_estimate=pl.CostEstimate(
            flops=20_000_000_000, bytes_accessed=4_000_000, transcendentals=0
        ),
    )(lengths, mixed_qkv, out_gate, beta_logit, step_logit, *small)


MESH = pl.DeviceIdType.MESH


def exchange_kernel(
    top_count, mixer_heads,
    input_ref, gain_ref, routes_ref, weights_ref, gate_ref, up_ref, down_ref,
    sgate_ref, sup_ref, sdown_ref, switch_ref,
    live_ref, qkv_ref, gate_in_ref, beta_ref, step_ref, taps_ref, log_ref, bias_ref, head_gain_ref,
    out_ref, core_ref,
    held, other_gate, other_up, other_down, hidden, shared_hidden, kept, staged,
    back_far, back_near, back_line,
    weight_send, weight_recv, line_send, near_send, far_send, held_recv,
    back_line_send, back_near_send, back_far_send,
    back_line_recv, back_near_recv, back_far_recv,
    run_t_ref, run_ref, strength_ref,
):
    tokens, features = input_ref.shape
    groups, expert = lax.axis_index("groups"), lax.axis_index("expert")
    cross, core = lax.axis_index("fsdp"), lax.axis_index("dp")
    line, side = expert // 2, expert % 2

    def device(line_at, side_at, cross_at, core_at):
        return (groups, line_at * 2 + side_at, cross_at, core_at)

    near = device(line, side + (1 - core) * (1 - 2 * side), cross + core * (1 - 2 * cross), core)
    far = device(line, side + core * (1 - 2 * side), cross + (1 - core) * (1 - 2 * cross), core)
    sibling = device(line, side, cross, 1 - core)
    places = (line, line + 1 - 2 * (line % 2), (line + 2) % 4, 3 - line)
    paired = [device(place, side, cross, core) for place in places]

    lane = lax.broadcasted_iota(jnp.int32, (tokens, 128), 1)
    per_core = gate_ref.shape[0]
    experts = 16 * per_core
    widened = input_ref[...].astype(jnp.float32)
    factor = lax.rsqrt(jnp.mean(widened * widened, axis=-1, keepdims=True) + EPS)
    held[0, :, 0:features] = (widened * factor * gain_ref[...]).astype(jnp.bfloat16)
    share = jnp.zeros((tokens, 128), jnp.float32)
    for choice in range(top_count):
        match = (lane % experts) == routes_ref[:, choice : choice + 1]
        share = share + jnp.where(match, weights_ref[:, choice : choice + 1], 0.0)
    high = share.astype(jnp.bfloat16).astype(jnp.float32)
    held[0, :, features : features + 128] = jnp.where(
        lane < experts, high, share - high
    ).astype(jnp.bfloat16)

    barrier = pltpu.get_barrier_semaphore()
    for partner in (near, far, sibling, paired[1], paired[2], paired[3]):
        pl.semaphore_signal(barrier, inc=1, device_id=partner, device_id_type=MESH)
    pl.semaphore_wait(barrier, 6)

    def send(source, target, send_sem, recv_sem, partner):
        copy = pltpu.make_async_remote_copy(
            src_ref=source, dst_ref=target, send_sem=send_sem, recv_sem=recv_sem,
            device_id=partner, device_id_type=MESH,
        )
        copy.start()
        return copy

    lines, nears, fars = {}, {}, {}

    def send_near(slot):
        nears[slot] = send(
            held.at[slot], held.at[4 + slot], near_send.at[slot], held_recv.at[4 + slot], near
        )

    def send_far(slot):
        fars[slot] = send(
            held.at[slot], held.at[8 + slot], far_send.at[slot], held_recv.at[8 + slot], far
        )

    def arrived(slot):
        if slot < 4:
            lines[slot].wait_recv()
        elif slot < 8:
            nears[slot - 4].wait_recv()
        else:
            fars[slot - 8].wait_recv()

    for step in (1, 3, 2):
        lines[step] = send(
            held.at[0], held.at[step], line_send.at[step], held_recv.at[step], paired[step]
        )
    send_near(0)
    send_far(0)
    exchanged = [
        send(source, target, weight_send.at[at], weight_recv.at[at], sibling)
        for at, (source, target) in enumerate(
            [(gate_ref, other_gate), (up_ref, other_up), (down_ref, other_down)]
        )
    ]

    def rows_of(slots):
        return jnp.concatenate([held[slot, :, 0:features] for slot in slots], axis=0)

    def share_of(slots, name):
        columns = [
            jnp.sum(
                jnp.where(
                    (lane == name) | (lane == name + experts),
                    held[slot, :, features : features + 128].astype(jnp.float32),
                    0.0,
                ),
                axis=1,
                keepdims=True,
            )
            for slot in slots
        ]
        return jnp.concatenate(columns, axis=0)

    def gated(rows, gate, up, scale):
        gate_part = jnp.dot(rows, gate, preferred_element_type=jnp.float32)
        up_part = jnp.dot(rows, up, preferred_element_type=jnp.float32)
        return (gate_part * sigmoid(gate_part) * up_part * scale).astype(jnp.bfloat16)

    width = gate_ref.shape[2]
    depth = per_core * width

    def experts_on(slots, with_shared):
        first = expert * (2 * per_core)

        @pl.loop(0, per_core)
        def _(index):
            rows = rows_of(slots)
            at = pl.multiple_of(index * width, width)
            hidden[:, pl.ds(at, width)] = gated(
                rows, gate_ref[index], up_ref[index],
                share_of(slots, first + core * per_core + index),
            )
            hidden[:, pl.ds(depth + at, width)] = gated(
                rows, other_gate[index], other_up[index],
                share_of(slots, first + (1 - core) * per_core + index),
            )

        if with_shared:
            scales = []
            for slot, live in zip(slots, (1, core, 1 - core, 0)):
                rows = held[slot, :, 0:features].astype(jnp.float32)
                total = jnp.sum(rows * switch_ref[...], axis=-1, keepdims=True)
                scales.append(sigmoid(total) * (jnp.zeros_like(total) + live))
            shared_hidden[...] = gated(
                rows_of(slots), sgate_ref[...], sup_ref[...], jnp.concatenate(scales, axis=0)
            )

        tile = 256

        @pl.loop(0, features // tile)
        def _(index):
            columns = pl.ds(pl.multiple_of(index * tile, tile), tile)
            total = jnp.dot(
                hidden[:, 0:depth], down_ref[:, columns], preferred_element_type=jnp.float32
            )
            total = total + jnp.dot(
                hidden[:, depth : 2 * depth], other_down[:, columns],
                preferred_element_type=jnp.float32,
            )
            if with_shared:
                total = total + jnp.dot(
                    shared_hidden[...], sdown_ref[:, columns], preferred_element_type=jnp.float32
                )
            for at, slot in enumerate(slots):
                part = total[at * tokens : (at + 1) * tokens]
                if slot < 8:
                    kept[slot, :, columns] = part
                else:
                    staged[slot, :, columns] = part.astype(jnp.bfloat16)

    back_fars, back_nears, back_lines = {}, {}, {}

    def return_far(slot):
        back_fars[slot] = send(
            staged.at[8 + slot], back_far.at[slot], back_far_send.at[slot],
            back_far_recv.at[slot], far,
        )

    def forward(slot):
        arrived(slot)
        send_near(slot)
        send_far(slot)

    def gather_near(slot):
        arrived(4 + slot)
        send_far(4 + slot)

    def run(slot):
        arrived(8 + slot)
        arrived(12 + slot)
        experts_on((slot, 4 + slot, 8 + slot, 12 + slot), slot == 0)
        return_far(4 + slot)
        return_far(slot)

    def reduce_near(slot):
        back_fars[4 + slot].wait_recv()
        staged[4 + slot] = (
            kept[4 + slot] + back_far[4 + slot].astype(jnp.float32)
        ).astype(jnp.bfloat16)
        back_nears[slot] = send(
            staged.at[4 + slot], back_near.at[slot], back_near_send.at[slot],
            back_near_recv.at[slot], near,
        )

    def reduce_line(slot):
        back_fars[slot].wait_recv()
        back_nears[slot].wait_recv()
        staged[slot] = (
            kept[slot] + back_far[slot].astype(jnp.float32) + back_near[slot].astype(jnp.float32)
        ).astype(jnp.bfloat16)
        back_lines[slot] = send(
            staged.at[slot], back_line.at[slot], back_line_send.at[slot],
            back_line_recv.at[slot], paired[slot],
        )

    def mix(start, stop):
        @pl.loop(start, stop)
        def _(group):
            mixer_group(
                group, 2, mixer_heads[0], mixer_heads[1], mixer_heads[2],
                qkv_ref, gate_in_ref, taps_ref, head_gain_ref, live_ref[0],
                run_t_ref, run_ref, strength_ref, core_ref,
            )

    mixer_prepare(beta_ref, step_ref, log_ref, bias_ref, run_t_ref, run_ref, strength_ref)
    gather_near(0)
    forward(1)
    mix(0, 1)
    gather_near(1)
    for copy in exchanged:
        copy.wait_recv()
    run(0)
    forward(3)
    mix(1, 2)
    gather_near(3)
    forward(2)
    run(1)
    gather_near(2)
    reduce_near(0)
    mix(2, 3)
    reduce_near(1)
    run(3)
    reduce_line(1)
    mix(3, mixer_heads[0] // 2)
    run(2)
    reduce_near(3)
    reduce_line(3)
    reduce_near(2)
    reduce_line(2)
    back_fars[0].wait_recv()
    back_nears[0].wait_recv()
    total = kept[0] + back_far[0].astype(jnp.float32) + back_near[0].astype(jnp.float32)
    for slot in (1, 3, 2):
        back_lines[slot].wait_recv()
        total = total + back_line[slot].astype(jnp.float32)
    out_ref[...] = total.astype(jnp.bfloat16)
    for copies in (lines, nears, fars, back_fars, back_nears, back_lines):
        for copy in copies.values():
            copy.wait_send()
    for copy in exchanged:
        copy.wait_send()


def exchanged_experts(
    moe_input, moe_gain, routes, route_gates, expert_gate, expert_up, expert_down,
    shared_gate, shared_up, shared_down, shared_switch,
    mixed_qkv, out_gate, beta_logit, step_logit, conv_weight, decay_log, decay_bias, head_gain, lengths,
):
    tokens, features = moe_input.shape
    _, length, channels = mixed_qkv.shape
    size = head_gain.shape[0]
    heads = decay_log.shape[0]
    key_heads = (channels - heads * size) // (2 * size)
    mixer_heads = (key_heads, heads // key_heads, size)
    vmem = pl.BlockSpec(memory_space=pltpu.VMEM)
    per_core, _, width = expert_gate.shape
    down = expert_down.reshape(per_core * width, features)
    block = (tokens, features)
    bf16, f32, dma = jnp.bfloat16, jnp.float32, pltpu.SemaphoreType.DMA
    moe_output, core_output = pl.pallas_call(
        functools.partial(exchange_kernel, routes.shape[1], mixer_heads),
        out_shape=[jax.ShapeDtypeStruct(block, bf16), jax.ShapeDtypeStruct(out_gate.shape[1:], bf16)],
        in_specs=[vmem] * 11 + [pl.BlockSpec(memory_space=pltpu.SMEM)] + [vmem] * 8,
        out_specs=[vmem, vmem],
        scratch_shapes=[
            pltpu.VMEM((16, tokens, features + 128), bf16),
            pltpu.VMEM(expert_gate.shape, bf16),
            pltpu.VMEM(expert_up.shape, bf16),
            pltpu.VMEM(down.shape, bf16),
            pltpu.VMEM((4 * tokens, 2 * per_core * width), bf16),
            pltpu.VMEM((4 * tokens, shared_gate.shape[1]), bf16),
            pltpu.VMEM((8,) + block, f32),
            pltpu.VMEM((16,) + block, bf16),
            pltpu.VMEM((8,) + block, bf16),
            pltpu.VMEM((4,) + block, bf16),
            pltpu.VMEM((4,) + block, bf16),
        ]
        + [dma((count,)) for count in (3, 3, 4, 4, 8, 16, 4, 4, 8, 4, 4, 8)]
        + [pltpu.VMEM((length, length), f32)] * 3,
        compiler_params=pltpu.CompilerParams(
            collective_id=0, has_side_effects=True, vmem_limit_bytes=56 * 1024 * 1024
        ),
        cost_estimate=pl.CostEstimate(
            flops=13_000_000_000, bytes_accessed=6_000_000, transcendentals=0
        ),
    )(
        moe_input, moe_gain[None, :], routes, route_gates, expert_gate, expert_up, down,
        shared_gate, shared_up, shared_down, shared_switch[None, :],
        lengths, mixed_qkv[0], out_gate[0], beta_logit[0], step_logit[0],
        conv_weight, decay_log[None, :], decay_bias[None, :], head_gain[None, :],
    )
    return moe_output, core_output[None]


def local(
    moe_input,
    moe_gain,
    routes,
    route_gates,
    expert_gate,
    expert_up,
    expert_down,
    shared_gate,
    shared_up,
    shared_down,
    shared_switch,
    mixed_qkv,
    out_gate,
    beta_logit,
    step_logit,
    conv_weight,
    decay_log,
    decay_bias,
    head_gain,
    lengths,
):
    sizes = (lax.axis_size("expert"), lax.axis_size("fsdp"), lax.axis_size("dp"))
    if sizes == (8, 2, 2) and mixed_qkv.shape[0] == 1:
        return exchanged_experts(
            moe_input, moe_gain, routes, route_gates, expert_gate, expert_up, expert_down,
            shared_gate, shared_up, shared_down, shared_switch,
            mixed_qkv, out_gate, beta_logit, step_logit, conv_weight, decay_log, decay_bias, head_gain, lengths,
        )
    core_output = mixer(
        mixed_qkv, out_gate, beta_logit, step_logit, conv_weight, decay_log, decay_bias, head_gain, lengths
    )
    normed = normalize_rows(moe_input, moe_gain).astype(jnp.bfloat16)
    tok_rows, top_count = routes.shape
    features = normed.shape[1]
    expert_count = lax.axis_size("expert")
    dp_count = lax.axis_size("dp")
    local_experts = expert_gate.shape[0]
    send_count = expert_count * dp_count
    all_experts = send_count * local_experts
    capacity = max(2, min(tok_rows, 5 * tok_rows * top_count // (4 * all_experts)))
    flat_routes = routes.reshape(-1)
    route_count = flat_routes.shape[0]
    one_hot = (flat_routes[:, None] == jnp.arange(all_experts, dtype=jnp.int32)[None, :]).astype(
        jnp.int32
    )
    earlier = jnp.cumsum(one_hot, axis=0) - one_hot
    rank_in = jnp.sum(earlier * one_hot, axis=1)
    slot_index = flat_routes * capacity + rank_in
    slot_tokens = (
        jnp.full((all_experts * capacity,), tok_rows, jnp.int32)
        .at[slot_index]
        .set(jnp.arange(route_count, dtype=jnp.int32) // top_count)
    )
    padded_rows = jnp.concatenate([normed, jnp.zeros((1, features), jnp.bfloat16)], axis=0)
    outgoing = padded_rows[slot_tokens]
    full_gate, full_up, full_down, whole_sgate, whole_sup, whole_sdown = (
        lax.all_gather(expert_gate, "fsdp", axis=2, tiled=True),
        lax.all_gather(expert_up, "fsdp", axis=2, tiled=True),
        lax.all_gather(expert_down, "fsdp", axis=1, tiled=True),
        lax.all_gather(shared_gate, "fsdp", axis=1, tiled=True),
        lax.all_gather(shared_up, "fsdp", axis=1, tiled=True),
        lax.all_gather(shared_down, "fsdp", axis=0, tiled=True),
    )
    shared_result = expert_rows(normed, whole_sgate, whole_sup, whole_sdown)
    switch = jax.nn.sigmoid(jnp.dot(normed.astype(jnp.float32), shared_switch, precision=HIGHEST))
    arrived = lax.all_to_all(
        outgoing.reshape(send_count, local_experts, capacity, features),
        ("expert", "dp"),
        split_axis=0,
        concat_axis=0,
        tiled=True,
    )
    gate_part = jnp.einsum("skcd,kdh->skch", arrived, full_gate, preferred_element_type=jnp.float32)
    up_part = jnp.einsum("skcd,kdh->skch", arrived, full_up, preferred_element_type=jnp.float32)
    hidden = (jax.nn.silu(gate_part) * up_part).astype(jnp.bfloat16)
    produced = jnp.einsum(
        "skch,khd->skcd", hidden, full_down, preferred_element_type=jnp.float32
    ).astype(jnp.bfloat16)
    returned = lax.all_to_all(produced, ("expert", "dp"), split_axis=0, concat_axis=0, tiled=True)
    returned = returned.reshape(all_experts * capacity, features)
    picked_rows = returned[slot_index].astype(jnp.float32).reshape(tok_rows, top_count, features)
    routed_sum = jnp.sum(route_gates[:, :, None] * picked_rows, axis=1)
    moe_output = (routed_sum + switch[:, None] * shared_result).astype(jnp.bfloat16)
    return (moe_output, core_output)


def solution(mesh):
    return jax.shard_map(
        local,
        mesh=mesh,
        in_specs=(
            P(("groups", "expert", "fsdp", "dp"), None),
            P(),
            P(("groups", "expert", "fsdp", "dp"), None),
            P(("groups", "expert", "fsdp", "dp"), None),
            P(("expert", "dp"), None, "fsdp"),
            P(("expert", "dp"), None, "fsdp"),
            P(("expert", "dp"), "fsdp", None),
            P(None, "fsdp"),
            P(None, "fsdp"),
            P("fsdp", None),
            P(),
            P(("groups", "expert", "fsdp", "dp"), None, None),
            P(("groups", "expert", "fsdp", "dp"), None, None),
            P(("groups", "expert", "fsdp", "dp"), None, None),
            P(("groups", "expert", "fsdp", "dp"), None, None),
            P(),
            P(),
            P(),
            P(),
            P(("groups", "expert", "fsdp", "dp")),
        ),
        out_specs=(
            P(("groups", "expert", "fsdp", "dp"), None),
            P(("groups", "expert", "fsdp", "dp"), None, None),
        ),
        check_vma=False,
    )
```
